32 devices in a mesh: groups: 2 (over x), ctx: 16 (over z, y, core).
Axes of the slice: x: 2, y: 2, z: 4, core: 2. Of those that a mesh axis runs over, the one named last changes fastest.
Arguments:
- features: bfloat16 [8192, 3, 4096], P(('groups', 'ctx')), parts along dimension 0, may hold values from -6 to 6
- short_weight: float32 [3, 3, 4096], replicated, may hold values from -3 to 3
- residues: float32 [256, 16], replicated, may hold values from -4 to 4
- rates: float32 [256, 16], replicated, may hold values from 0 to 1, as said below
- skip: float32 [4096], replicated, may hold values from -4 to 4
- carry_state: float32 [32, 4096], P('groups'), parts along dimension 0, may hold values from -120 to 120
- earlier_rows: bfloat16 [4, 3, 4096], P('groups'), parts along dimension 0, may hold values from -6 to 6
- segment_ids: int32 [8192], P('groups'), parts along dimension 0, may hold values from 0 to 7, never falling along the last dimension, each value on 1 to 3072 neighbouring positions
Outputs:
- mixed: bfloat16 [8192, 4096], P(('groups', 'ctx')), parts along dimension 0
The draws below stay inside these ranges and needn't reach their ends.
There are 2 independent parts, one for each index of `groups`. The reference program is written for one: setup_inputs(seed, part) draws one part's arguments, and reference() takes and returns one part's arrays. A program takes and returns all parts, laid end to end along the dimension named above; an argument that names none is the same for every part. Nothing has to cross between parts.
Inputs may be any that keep to these rules, and one draw needn't show every extreme that they name: Positive decay rates, at most 1 / 30. `segment_ids`: never falling, starting at record 0, which continues the record that closes the earlier span; each record holds at most 3072 tokens, one exactly that many.
All inputs are finite; a program needn't handle non-finite values.
Results may differ from the reference program's by a relative error of at most 0.0065.
Values may be sent and summed in bfloat16 or wider, within the bound.
A program may use at most 128 MiB of HBM per device.

```python
import math
import jax
import jax.numpy as jnp
import numpy as np
from jax import lax

CH = 4096
FG = 16
MODES = 16
TAPS = 3
SEGS = 8
TOK_DEV = 256
GRP = 256
SEQ = 4096
N_CTX = 16


def draw_rates(key, part):
    key_slow, key_fast, key_pick = jax.random.split(jax.random.fold_in(key, 17), 3)
    shape = (CH // FG, MODES)
    slow = jnp.exp(jax.random.uniform(key_slow, shape, jnp.float32, jnp.log(0.2 / SEQ), jnp.log(2.0 / SEQ)))
    fast = jnp.exp(jax.random.uniform(key_fast, shape, jnp.float32, jnp.log(1.0 / 50.0), jnp.log(1.0 / 30.0)))
    share = 0.5
    pick = jax.random.uniform(key_pick, shape, jnp.float32) < share
    return jnp.where(pick, slow, fast).astype(jnp.float32)


def block_levels(rng, shape, cuts, low, top_value):
    loudness, own = 1.0, jax.random.fold_in(rng, 6)
    for axis_at, parts in cuts:
        draws = jnp.exp(jax.random.uniform(jax.random.fold_in(own, axis_at), (parts,), jnp.float32, low / len(cuts), top_value / len(cuts)))
        loudness = loudness * jnp.repeat(draws, shape[axis_at] // parts).reshape([-1 if axis == axis_at else 1 for axis in range(len(shape))])
    return loudness


def split_up(count, total, bound, slope):
    portions = [(1 << 20) // math.isqrt(grade ** slope) + 1 for grade in range(2, count + 1)]
    surplus, holding = total - bound - (count - 1), [1] * (count - 1)
    while surplus > 0:
        candidates = [i for i in range(count - 1) if holding[i] < bound]
        whole, budget = sum([portions[i] for i in candidates]), surplus
        for i in candidates:
            more = min(bound - holding[i], max(1, budget * portions[i] // whole), surplus)
            holding[i] = holding[i] + more
            surplus = surplus - more
    return np.array([bound] + holding)


def ragged(rng, count, total, bound, skew):
    if count == 2:
        one = jax.random.randint(rng, (), max(1, total - bound), min(bound, total - 1) + 1)
        return jnp.stack([one, total - one])
    lengths = jnp.asarray(split_up(count, total, bound, skew), jnp.int32)
    twos = (count - 1) // 2
    source_of, sink = lengths[1:1 + 2 * twos:2], lengths[2:2 + 2 * twos:2]
    margin = jnp.minimum(source_of - 1, bound - sink)
    shifted = jax.random.randint(jax.random.fold_in(rng, 1), (twos,), 0, 1 << 20) % (margin + 1)
    lengths = lengths.at[1:1 + 2 * twos:2].set(source_of - shifted).at[2:2 + 2 * twos:2].set(sink + shifted)
    return lengths[jax.random.permutation(jax.random.fold_in(rng, 2), count)]


def gaussian(key, extent, scale, bound, pieces=(), dtype=jnp.bfloat16):
    entries = scale * jax.random.normal(key, extent, jnp.float32)
    if pieces:
        entries = entries * block_levels(key, extent, pieces, -0.22, 0.18)
    return jnp.clip(entries, -bound, bound).astype(dtype)


def setup_inputs(seed: int = 0, part: int = 0) -> dict:
    streams_of = jax.random.split(jax.random.key(seed), 9)
    part_splits = jax.random.split(jax.random.fold_in(streams_of[8], part), 9)
    features = gaussian(part_splits[0], (SEQ, 3, CH), 1.0, 6.0, ((0, 16),))
    short_weight = gaussian(streams_of[1], (TAPS, 3, CH), 0.6, 3.0, (), jnp.float32)
    residues = gaussian(streams_of[2], (GRP, MODES), 1.0, 4.0, (), jnp.float32)
    rates = draw_rates(jax.random.fold_in(streams_of[8], 71), part)
    skip = gaussian(streams_of[4], (CH,), 1.0, 4.0, (), jnp.float32)
    carry_state = gaussian(part_splits[5], (MODES, CH), 20.0, 120.0, (), jnp.float32)
    earlier_rows = gaussian(part_splits[6], (2, 3, CH), 1.0, 6.0)
    segment_ids = jnp.searchsorted(jnp.cumsum(ragged(part_splits[7], SEGS, SEQ, SEQ - SEQ // 4, 2)), jnp.arange(SEQ), side="right").astype(jnp.int32)
    return {"features": features, "short_weight": short_weight, "residues": residues, "rates": rates, "skip": skip, "carry_state": carry_state, "earlier_rows": earlier_rows, "segment_ids": segment_ids}


def short_filter(rows_ext, short_weight, seg_ext):
    count = rows_ext.shape[0] - 2
    total = jnp.zeros((count,) + rows_ext.shape[1:], jnp.float32)
    for offset in range(short_weight.shape[0]):
        begin = 2 - offset
        piece = rows_ext[begin:begin + count].astype(jnp.float32)
        keep = seg_ext[begin:begin + count] == seg_ext[2:]
        total = total + short_weight[offset][None] * jnp.where(keep[:, None, None], piece, jnp.float32(0.0))
    return total

def lag_table(residues, rates, count):
    lags = jnp.arange(count).astype(jnp.float32)
    weight_mode = residues * jnp.sqrt(rates)
    return lax.optimization_barrier(jnp.sum(weight_mode[:, :, None] * jnp.exp(-rates[:, :, None] * lags[None, None, :]), axis=1))

def toeplitz(table):
    count = table.shape[1]
    flipped = jnp.concatenate([table[:, ::-1], jnp.zeros_like(table)], axis=1)
    tiled = jnp.tile(flipped, (1, count + 1))
    window = tiled[:, count - 1:count - 1 + count * (2 * count - 1)]
    return window.reshape(table.shape[0], count, 2 * count - 1)[:, :, :count]

def local_conv(u_block, seg_blk, table):
    count, width = u_block.shape
    groups = table.shape[0]
    members = width // groups
    step_groups = min(groups, 16)
    rounds = groups // step_groups
    same = seg_blk[:, None] == seg_blk[None, :]
    grouped = u_block.reshape(count, rounds, step_groups, members).transpose(1, 0, 2, 3)
    tables = table.reshape(rounds, step_groups, count)

    def one_step(pair):
        tab, values = pair
        matrix = jnp.where(same[None], toeplitz(tab), jnp.float32(0.0))
        matrix = lax.optimization_barrier(matrix.astype(jnp.bfloat16)).astype(jnp.float32)
        return jnp.einsum('gts,sgf->tgf', matrix, values.astype(jnp.float32), precision=lax.Precision.HIGHEST)
    result = lax.map(one_step, (tables, grouped))
    return result.transpose(1, 0, 2, 3).reshape(count, width)

def block_state(u_block, seg_blk, seg_prev, rates):
    count, width = u_block.shape
    groups = rates.shape[0]
    members = width // groups
    lags_end = (count - 1 - jnp.arange(count)).astype(jnp.float32)
    keep_end = seg_blk == seg_blk[count - 1]
    decay = jnp.where(keep_end[None, None, :], jnp.exp(-rates[:, :, None] * lags_end[None, None, :]), jnp.float32(0.0))
    decay = lax.optimization_barrier(decay.astype(jnp.bfloat16)).astype(jnp.float32)
    grouped = u_block.reshape(count, groups, members).astype(jnp.float32)
    block_sum = jnp.einsum('gms,sgf->mgf', decay, grouped, precision=lax.Precision.HIGHEST)
    factor = jnp.where(seg_prev == seg_blk[count - 1], jnp.exp(-rates * count), jnp.float32(0.0))
    return (factor.T[:, :, None], block_sum)

def cross_term(state_in, seg_blk, seg_prev, residues, rates):
    count = seg_blk.shape[0]
    offsets = jnp.arange(1, count + 1).astype(jnp.float32)
    weights = (residues * jnp.sqrt(rates))[None] * jnp.exp(-rates[None] * offsets[:, None, None])
    weights = jnp.where((seg_blk == seg_prev)[:, None, None], weights, jnp.float32(0.0))
    result = jnp.einsum('tgm,mgf->tgf', weights, state_in, precision=lax.Precision.HIGHEST)
    return result.reshape(count, -1)

def reference(features, short_weight, residues, rates, skip, carry_state, earlier_rows, segment_ids):
    count = TOK_DEV
    groups, modes = rates.shape
    width = features.shape[2]
    members = width // groups
    table = lag_table(residues, rates, count)
    seg_pad = jnp.concatenate([jnp.zeros((2,), jnp.int32), segment_ids.astype(jnp.int32)])
    blocks = features.reshape(N_CTX, count, 3, width)

    def advance(carry, inputs):
        state, previous = carry
        rows, number = inputs
        seg_ext = lax.dynamic_slice(seg_pad, (number * count,), (count + 2,))
        seg_blk = seg_ext[2:]
        seg_prev = seg_ext[1]
        extended = jnp.concatenate([previous, rows], axis=0)
        filtered = short_filter(extended, short_weight, seg_ext)
        u_block = lax.optimization_barrier((filtered[:, 1] * filtered[:, 2]).astype(jnp.bfloat16))
        local = local_conv(u_block, seg_blk, table)
        factor, block_sum = block_state(u_block, seg_blk, seg_prev, rates)
        cross = cross_term(state, seg_blk, seg_prev, residues, rates)
        mixed = (filtered[:, 0] * (local + cross + skip[None] * u_block.astype(jnp.float32))).astype(jnp.bfloat16)
        return ((factor * state + block_sum, rows[count - 2:]), mixed)
    numbers = jnp.arange(N_CTX).astype(jnp.int32)
    start_state = (carry_state.reshape(modes, groups, members), earlier_rows)
    final, outputs = lax.scan(advance, start_state, (blocks, numbers))
    return outputs.reshape(N_CTX * count, width)
```

```python
import functools

import jax
import jax.numpy as jnp
from jax import lax
from jax.experimental import pallas as pl
from jax.experimental.pallas import tpu as pltpu
from jax.sharding import PartitionSpec as P

F32 = jnp.float32
BF16 = jnp.bfloat16
L = 128
W = 256
MODES = 16
FG = 16
GT = W // FG


def column(row):
    return jnp.transpose(jnp.broadcast_to(row, (row.shape[1], row.shape[1])))


def segment_tables(seg_ref, block, mask_ref, near_ref, cmask_ref, dmask_ref):
    rows = [seg_ref[pl.ds(2 * block + j, 1), :] for j in range(2)]
    before = seg_ref[pl.ds(jnp.maximum(2 * block - 1, 0), 1), :]
    before = jnp.where(block == 0, jnp.zeros_like(before), before)
    lane = lax.broadcasted_iota(jnp.int32, (1, L), 1)
    t_at = lax.broadcasted_iota(jnp.int32, (L, L), 0)
    s_at = lax.broadcasted_iota(jnp.int32, (L, L), 1)
    for j in range(2):
        row = rows[j]
        last = before if j == 0 else rows[0]
        one, two = last[:, L - 1 : L], last[:, L - 2 : L - 1]
        prev1 = jnp.where(lane == 0, one, pltpu.roll(row, 1, 1))
        prev2 = jnp.where(lane == 0, two, jnp.where(lane == 1, one, pltpu.roll(row, 2, 1)))
        near_ref[0, j * L : (j + 1) * L, :] = column((prev1 == row).astype(F32))
        near_ref[1, j * L : (j + 1) * L, :] = column((prev2 == row).astype(F32))
        cmask_ref[j * L : (j + 1) * L, :] = column((row == one).astype(F32))
        dmask_ref[j : j + 1, :] = (row == row[:, L - 1 : L]).astype(F32)
        seg_t = column(row.astype(F32))
        keep = (seg_t == row.astype(F32)) & (t_at >= s_at)
        mask_ref[j * L : (j + 1) * L, :] = keep.astype(F32).astype(BF16)
    keep0 = (rows[0][:, L - 1 : L] == before[:, L - 1 : L]).astype(F32)
    keep1 = (rows[1][:, L - 1 : L] == rows[0][:, L - 1 : L]).astype(F32)
    return keep0, keep1


def block_diagonal():
    r = lax.broadcasted_iota(jnp.int32, (W, W), 0) // FG
    c = lax.broadcasted_iota(jnp.int32, (W, W), 1) // FG
    return (r == c).astype(F32)


def wide(mask):
    return jnp.concatenate([mask, mask], axis=1)


def short_filter(x, prev, taps, near_ref):
    row = lax.broadcasted_iota(jnp.int32, (8, W), 0)
    x1 = pltpu.roll(x, 1, 0)
    x2 = pltpu.roll(x, 2, 0)
    h1 = jnp.where(row == 0, prev[1:2], x1[:8])
    h2 = jnp.where(row == 0, prev[0:1], jnp.where(row == 1, prev[1:2], x2[:8]))
    x1 = jnp.concatenate([h1, x1[8:]], axis=0)
    x2 = jnp.concatenate([h2, x2[8:]], axis=0)
    return taps[0:1] * x + wide(near_ref[0]) * (taps[1:2] * x1) + wide(near_ref[1]) * (taps[2:3] * x2)


def rate_columns(rate_row, weight_row):
    turn = lambda r: jnp.transpose(jnp.broadcast_to(r, (L, W)))
    return turn(rate_row), turn(weight_row)


def end_decay(rate_col):
    lag = (L - 1) - lax.broadcasted_iota(jnp.int32, (W, L), 1)
    return jnp.exp(-rate_col * lag.astype(F32))


def fold(full, diag):
    return jnp.sum((full * diag).reshape(GT, MODES, W), axis=0)


def spread(state, diag16):
    return jnp.concatenate([state] * GT, axis=0) * diag16


def cross_weights(rate_row, weight_row):
    step = lax.broadcasted_iota(jnp.int32, (L, W), 0) + 1
    return weight_row * jnp.exp(-rate_row * step.astype(F32))


def mm(a, b):
    return lax.dot_general(a, b, (((1,), (0,)), ((), ())), preferred_element_type=F32)


def local_tile(u, decay, weight_col, mask_ref, diag16, big_ref, val_ref):
    table = jnp.sum((weight_col * decay).reshape(GT, MODES, L), axis=1)
    table = pltpu.roll(table, 1, 1)
    for g in range(GT):
        square = jnp.broadcast_to(table[g : g + 1], (L, L))
        square = pltpu.roll(square, 0, 1, stride=1, stride_axis=0).astype(BF16)
        lanes = jnp.concatenate([diag16[g * FG : (g + 1) * FG]] * (L // FG), axis=0)
        for j in range(2):
            big_ref[j, :, g * L : (g + 1) * L] = square * mask_ref[j * L : (j + 1) * L, :]
            val_ref[j, g * L : (g + 1) * L, :] = u[j * L : (j + 1) * L] * lanes
    return [mm(big_ref[j], val_ref[j]) for j in range(2)]


def first_kernel(seg_ref, feat_ref, prev_ref, taps_ref, skip_ref, rate_ref, weight_ref, part_ref, q_ref, sum_ref,
                 mask_ref, near_ref, cmask_ref, dmask_ref, diag_ref, diag16_ref, big_ref, val_ref, keep_ref):
    block = lax.axis_index("ctx")

    @pl.when(pl.program_id(0) == 0)
    def _():
        keep0, keep1 = segment_tables(seg_ref, block, mask_ref, near_ref, cmask_ref, dmask_ref)
        keep_ref[...] = jnp.broadcast_to(keep1, keep_ref.shape)
        diag = block_diagonal()
        diag_ref[...] = diag
        diag16_ref[...] = diag.astype(BF16)

    filt = [
        short_filter(feat_ref[i].astype(F32), prev_ref[i].astype(F32), taps_ref[:, i], near_ref) for i in range(3)
    ]
    u = (filt[1] * filt[2]).astype(BF16)
    rate_row, weight_row = rate_ref[...], weight_ref[...]
    rate_col, weight_col = rate_columns(rate_row, weight_row)
    decay = end_decay(rate_col)
    sums = [
        fold(mm((decay * dmask_ref[j : j + 1]).astype(BF16), u[j * L : (j + 1) * L]), diag_ref[...]) for j in range(2)
    ]
    rate_mc = fold(wide(rate_col), diag_ref[...])
    sum_ref[...] = keep_ref[0:1, 0:1] * jnp.exp(-rate_mc * L) * sums[0] + sums[1]
    diag16 = diag16_ref[...]
    local = local_tile(u, decay, weight_col, mask_ref, diag16, big_ref, val_ref)
    weights = (cross_weights(rate_row, weight_row) * wide(cmask_ref[L:, :])).astype(BF16)
    local[1] = local[1] + mm(weights, spread(sums[0].astype(BF16), diag16))
    for j in range(2):
        at = slice(j * L, (j + 1) * L)
        part_ref[at, :] = (local[j] + skip_ref[...] * u[at].astype(F32)).astype(part_ref.dtype)
        q_ref[at, :] = filt[0][at].astype(q_ref.dtype)


def second_kernel(seg_ref, part_ref, q_ref, state_ref, rate_ref, weight_ref, out_ref,
                  mask_ref, near_ref, cmask_ref, dmask_ref, diag_ref, keep_ref):
    block = lax.axis_index("ctx")

    @pl.when(pl.program_id(0) == 0)
    def _():
        keep0, keep1 = segment_tables(seg_ref, block, mask_ref, near_ref, cmask_ref, dmask_ref)
        keep_ref[...] = jnp.broadcast_to(keep0, keep_ref.shape)
        diag_ref[...] = block_diagonal()

    rate_row, weight_row = rate_ref[...], weight_ref[...]
    rate_col, _ = rate_columns(rate_row, weight_row)
    weights = cross_weights(rate_row, weight_row)
    rate_mc = fold(wide(rate_col), diag_ref[...])
    state = state_ref[...]
    later = keep_ref[0:1, 0:1] * jnp.exp(-rate_mc * L) * state
    diag16 = diag_ref[...].astype(BF16)
    for j, held in enumerate((state, later)):
        at = slice(j * L, (j + 1) * L)
        cross = mm((weights * wide(cmask_ref[at, :])).astype(BF16), spread(held.astype(BF16), diag16))
        out_ref[at, :] = (q_ref[at, :].astype(F32) * (part_ref[at, :].astype(F32) + cross)).astype(BF16)


def body(features, short_weight, residues, rates, skip, carry_state, earlier_rows, segment_ids):
    count, _, width = features.shape
    groups, modes = rates.shape
    tiles = width // W
    position = lax.axis_index("ctx")
    n = lax.axis_size("ctx")
    feat = features.transpose(1, 0, 2)
    tail = lax.ppermute(feat[:, count - 2 :], "ctx", [(i, i + 1) for i in range(n - 1)])
    prev = jnp.where(position == 0, earlier_rows.transpose(1, 0, 2), tail)
    seg = segment_ids.reshape(-1, L)
    rate_row = rates.reshape(1, -1)
    weight_row = (residues * jnp.sqrt(rates)).reshape(1, -1)
    skip_row = skip.reshape(1, -1)
    whole = lambda shape: pl.BlockSpec(shape, lambda i: (0,) * len(shape))
    row_spec = pl.BlockSpec((1, W), lambda i: (0, i))
    tok_spec = pl.BlockSpec((count, W), lambda i: (0, i))
    mode_spec = pl.BlockSpec((modes, W), lambda i: (0, i))
    seg_scratch = [
        pltpu.VMEM((count, L), BF16),
        pltpu.VMEM((2, count, L), F32),
        pltpu.VMEM((count, L), F32),
        pltpu.VMEM((8, L), F32),
    ]
    params = pltpu.CompilerParams(vmem_limit_bytes=48 * 1024 * 1024)
    part, q, sums = pl.pallas_call(
        first_kernel,
        grid=(tiles,),
        in_specs=[
            whole(seg.shape),
            pl.BlockSpec((3, count, W), lambda i: (0, 0, i)),
            pl.BlockSpec((3, 2, W), lambda i: (0, 0, i)),
            pl.BlockSpec((3, 3, W), lambda i: (0, 0, i)),
            row_spec, row_spec, row_spec,
        ],
        out_specs=[tok_spec, tok_spec, mode_spec],
        out_shape=[
            jax.ShapeDtypeStruct((count, width), F32),
            jax.ShapeDtypeStruct((count, width), F32),
            jax.ShapeDtypeStruct((modes, width), F32),
        ],
        scratch_shapes=seg_scratch + [
            pltpu.VMEM((W, W), F32),
            pltpu.VMEM((W, W), BF16),
            pltpu.VMEM((2, L, GT * L), BF16),
            pltpu.VMEM((2, GT * L, W), BF16),
            pltpu.VMEM((8, L), F32),
        ],
        compiler_params=params,
        name="local",
    )(seg, feat, prev, short_weight, skip_row, rate_row, weight_row)

    piece = lax.all_gather(sums.astype(BF16), "ctx", axis=0)
    owners = jnp.arange(n, dtype=jnp.int32)
    ends = segment_ids.reshape(n, count)[:, count - 1]
    seg_prev = jnp.where(position == 0, 0, ends[jnp.maximum(position - 1, 0)])
    distance = jnp.maximum(position - 1 - owners, 0).astype(F32)
    usable = (owners < position) & (ends == seg_prev)
    rate_mc = jnp.repeat(rates.T, FG, axis=1)
    factor = jnp.where(usable[:, None, None], jnp.exp(-rate_mc[None] * count * distance[:, None, None]), F32(0.0))
    lead = jnp.where(seg_prev == 0, jnp.exp(-rate_mc * (count * position).astype(F32)), F32(0.0))
    state = lead * carry_state + jnp.sum(factor * piece.astype(F32), axis=0)

    return pl.pallas_call(
        second_kernel,
        grid=(tiles,),
        in_specs=[whole(seg.shape), tok_spec, tok_spec, mode_spec, row_spec, row_spec],
        out_specs=tok_spec,
        out_shape=jax.ShapeDtypeStruct((count, width), BF16),
        scratch_shapes=seg_scratch + [pltpu.VMEM((W, W), F32), pltpu.VMEM((8, L), F32)],
        compiler_params=params,
        name="cross",
    )(seg, part, q, state, rate_row, weight_row)


def solution(mesh):
    placed = (
        P(("groups", "ctx"), None, None),
        P(),
        P(),
        P(),
        P(),
        P("groups", None),
        P("groups", None, None),
        P("groups"),
    )
    return jax.shard_map(
        body, mesh=mesh, in_specs=placed, out_specs=P(("groups", "ctx"), None), check_vma=False
    )
```

```python
import functools

import jax
import jax.numpy as jnp
from jax import lax
from jax.experimental import pallas as pl
from jax.experimental.pallas import tpu as pltpu
from jax.sharding import PartitionSpec as P

F32 = jnp.float32
BF16 = jnp.bfloat16
L = 128
W = 256
MODES = 16
FG = 16
GT = W // FG
G = 4
FW = 512


def column(row):
    return jnp.transpose(jnp.broadcast_to(row, (row.shape[1], row.shape[1])))


def segment_tables(seg_ref, block, mask_ref, near_ref, cmask_ref, dmask_ref):
    rows = [seg_ref[pl.ds(2 * block + j, 1), :] for j in range(2)]
    before = seg_ref[pl.ds(jnp.maximum(2 * block - 1, 0), 1), :]
    before = jnp.where(block == 0, jnp.zeros_like(before), before)
    lane = lax.broadcasted_iota(jnp.int32, (1, L), 1)
    t_at = lax.broadcasted_iota(jnp.int32, (L, L), 0)
    s_at = lax.broadcasted_iota(jnp.int32, (L, L), 1)
    for j in range(2):
        row = rows[j]
        last = before if j == 0 else rows[0]
        one, two = last[:, L - 1 : L], last[:, L - 2 : L - 1]
        prev1 = jnp.where(lane == 0, one, pltpu.roll(row, 1, 1))
        prev2 = jnp.where(lane == 0, two, jnp.where(lane == 1, one, pltpu.roll(row, 2, 1)))
        near_ref[0, j * L : (j + 1) * L, :] = column((prev1 == row).astype(F32))
        near_ref[1, j * L : (j + 1) * L, :] = column((prev2 == row).astype(F32))
        cmask_ref[j * L : (j + 1) * L, :] = column((row == one).astype(F32))
        dmask_ref[j : j + 1, :] = (row == row[:, L - 1 : L]).astype(F32)
        seg_t = column(row.astype(F32))
        keep = (seg_t == row.astype(F32)) & (t_at >= s_at)
        mask_ref[j * L : (j + 1) * L, :] = keep.astype(F32).astype(BF16)
    keep0 = (rows[0][:, L - 1 : L] == before[:, L - 1 : L]).astype(F32)
    keep1 = (rows[1][:, L - 1 : L] == rows[0][:, L - 1 : L]).astype(F32)
    return keep0, keep1


def block_diagonal():
    r = lax.broadcasted_iota(jnp.int32, (W, W), 0) // FG
    c = lax.broadcasted_iota(jnp.int32, (W, W), 1) // FG
    return (r == c).astype(F32)


def wide(mask):
    return jnp.concatenate([mask, mask], axis=1)


def short_filter(x, prev, taps, near_ref):
    row = lax.broadcasted_iota(jnp.int32, (8, W), 0)
    x1 = pltpu.roll(x, 1, 0)
    x2 = pltpu.roll(x, 2, 0)
    h1 = jnp.where(row == 0, prev[1:2], x1[:8])
    h2 = jnp.where(row == 0, prev[0:1], jnp.where(row == 1, prev[1:2], x2[:8]))
    x1 = jnp.concatenate([h1, x1[8:]], axis=0)
    x2 = jnp.concatenate([h2, x2[8:]], axis=0)
    return taps[0:1] * x + wide(near_ref[0]) * (taps[1:2] * x1) + wide(near_ref[1]) * (taps[2:3] * x2)


def end_decay(rate_col):
    lag = (L - 1) - lax.broadcasted_iota(jnp.int32, (W, L), 1)
    return jnp.exp(-rate_col * lag.astype(F32))


def fold(full, diag):
    return jnp.sum((full * diag).reshape(GT, MODES, W), axis=0)


def spread(state, diag16):
    return jnp.concatenate([state] * GT, axis=0) * diag16


def mm(a, b):
    return lax.dot_general(a, b, (((1,), (0,)), ((), ())), preferred_element_type=F32)


def kernel(n, seg_ref, feat_hbm, earlier_ref, taps_ref, skip_ref, rate_ref, res_ref, carry_ref, out_hbm,
           feat, tail16, pack, got, prev, mask_ref, near_ref, cmask_ref, dmask_ref, diag_ref, diag16_ref, keep_ref,
           dec, cw, hs, a128, u_ref, q_ref, part, s0_ref, sumq, b_ref, x_ref, xr, acc, s3, sin, big, val, outb,
           fsem, tsem, tail_send, tail_recv, s1_send, s1_recv, x_send, x_recv, s3_send, s3_recv, osem):
    count, width = u_ref.shape
    tiles = width // W
    wq = width // G
    per = wq // W
    planes = n // G
    p = lax.axis_index("ctx")
    i, z = p % G, p // G

    def lanes(t, size=W):
        return pl.ds(pl.multiple_of(t * size, size), size)

    def fetch(t):
        return pltpu.make_async_copy(feat_hbm.at[:, :, lanes(t, FW)], feat.at[:, :, lanes(t, FW)], fsem.at[t])

    def remote(src, dst, send, recv, target):
        return pltpu.make_async_remote_copy(
            src_ref=src, dst_ref=dst, send_sem=send, recv_sem=recv,
            device_id={"ctx": target}, device_id_type=pl.DeviceIdType.MESH,
        )

    barrier = pltpu.get_barrier_semaphore()

    def greet(d, c):
        pl.semaphore_signal(barrier, inc=1, device_id={"ctx": (p + d) % n}, device_id_type=pl.DeviceIdType.MESH)
        return c

    lax.fori_loop(1, n, greet, 0)
    rows16 = pltpu.make_async_copy(feat_hbm.at[:, pl.ds(count - 16, 16), :], tail16, tsem)
    rows16.start()
    lax.fori_loop(0, width // FW, lambda t, c: (fetch(t).start(), c)[1], 0)

    keep0, keep1 = segment_tables(seg_ref, p, mask_ref, near_ref, cmask_ref, dmask_ref)
    keep_ref[0:8, :] = jnp.broadcast_to(keep0, (8, L))
    keep_ref[8:16, :] = jnp.broadcast_to(keep1, (8, L))
    diag = block_diagonal()
    diag_ref[...] = diag
    diag16_ref[...] = diag.astype(BF16)

    half = width // 2
    rows16.wait()
    pieces = []
    for a in range(3):
        last = tail16[a].astype(F32)[14:16]
        pieces += [last[:, :half], last[:, half:]]
    pack[...] = jnp.concatenate(pieces + [jnp.zeros((4, half), F32)], axis=0).astype(BF16)
    pl.semaphore_wait(barrier, n - 1)
    tail_copy = remote(pack, got, tail_send, tail_recv, (p + 1) % n)

    @pl.when(p < n - 1)
    def _():
        tail_copy.start()

    weight_mg = res_ref[...] * jnp.sqrt(rate_ref[...])

    def tables(t):
        back = (rate_ref.shape[1] - GT * t) % rate_ref.shape[1]
        rates = pltpu.roll(rate_ref[...], back, 1)
        weights = pltpu.roll(weight_mg, back, 1)
        spell = lambda v: jnp.concatenate(
            [jnp.broadcast_to(v[:, g : g + 1], (MODES, L)) for g in range(GT)], axis=0)
        rate_col, weight_col = spell(rates), spell(weights)
        decay = end_decay(rate_col)
        rows = lanes(t)
        for j in range(2):
            dec[j, rows, :] = (decay * dmask_ref[j : j + 1]).astype(BF16)
        table = jnp.sum((weight_col * decay).reshape(GT, MODES, L), axis=1)
        hs[lanes(t, GT), :] = pltpu.roll(table, 1, 1)
        step = lax.broadcasted_iota(jnp.int32, (W, L), 1) + 1
        cross = jnp.transpose(weight_col * jnp.exp(-rate_col * step.astype(F32)))
        for j in range(2):
            cw[j * L : (j + 1) * L, rows] = (cross * wide(cmask_ref[j * L : (j + 1) * L, :])).astype(BF16)
        a128[t // per, :, lanes(t % per)] = jnp.exp(-L * fold(wide(rate_col), diag_ref[...]))

    def pairs(begin, end, step):
        def both(t2, c):
            step(2 * t2, 0)
            step(2 * t2 + 1, 1)
            return c
        lax.fori_loop(begin // 2, end // 2, both, 0)

    pairs(0, tiles, lambda t, slot: tables(t))

    @pl.when(p == 0)
    def _():
        for a in range(3):
            prev[a, 0:2, :] = earlier_ref[a].astype(F32)

    @pl.when(p > 0)
    def _():
        tail_copy.wait_recv()
        rows = got[...].astype(F32)
        for a in range(3):
            for h in range(2):
                prev[a, 0:2, h * half : (h + 1) * half] = rows[4 * a + 2 * h : 4 * a + 2 * h + 2]

    lax.fori_loop(0, width // FW, lambda t, c: (fetch(t).wait(), c)[1], 0)

    def filtered(a, at):
        return short_filter(feat[a, :, at].astype(F32), prev[a, 0:2, at], taps_ref[:, a, at], near_ref)

    def sums(t):
        at = lanes(t)
        u = (filtered(1, at) * filtered(2, at)).astype(BF16)
        u_ref[:, at] = u
        both = [fold(mm(dec[j, at, :], u[j * L : (j + 1) * L]), diag_ref[...]) for j in range(2)]
        s0_ref[:, at] = both[0]
        total = keep_ref[8:9, 0:1] * a128[t // per, :, lanes(t % per)] * both[0] + both[1]
        sumq[t // per, :, lanes(t % per)] = total.astype(BF16)

    pairs(0, tiles, lambda t, slot: sums(t))

    def to_mate(d):
        k = (i + d) % G
        return remote(sumq.at[k], b_ref.at[i], s1_send.at[d], s1_recv.at[i], z * G + k)

    def from_mate(d):
        k = (i + d) % G
        return remote(sumq.at[k], b_ref.at[k], s1_send.at[d], s1_recv.at[k], z * G + k)

    for d in range(1, G):
        to_mate(d).start()
    b_ref[i] = sumq[i]

    def local(t, slot):
        at = lanes(t)
        u = u_ref[:, at]
        table = hs[lanes(t, GT), :]
        for g in range(GT):
            square = jnp.broadcast_to(table[g : g + 1], (L, L))
            square = pltpu.roll(square, 0, 1, stride=1, stride_axis=0).astype(BF16)
            own = jnp.concatenate([diag16_ref[g * FG : (g + 1) * FG, :]] * (L // FG), axis=0)
            for j in range(2):
                big[slot, j, :, g * L : (g + 1) * L] = square * mask_ref[j * L : (j + 1) * L, :]
                val[slot, j, g * L : (g + 1) * L, :] = u[j * L : (j + 1) * L] * own
        for j in range(2):
            part[j * L : (j + 1) * L, at] = (
                mm(big[slot, j], val[slot, j]) + skip_ref[:, at] * u[j * L : (j + 1) * L].astype(F32))
        q_ref[:, at] = filtered(0, at)

    cuts = [0, tiles // 4 // 2 * 2, 3 * tiles // 4 // 2 * 2, tiles]
    pairs(cuts[0], cuts[1], local)

    def end_of(block):
        return seg_ref[pl.ds(jnp.maximum(2 * block + 1, 0), 1), L - 1 : L]

    def same(one, two):
        return (one == two).astype(F32)

    ends = [end_of(z * G + k) for k in range(G)]
    entry = end_of(z * G - 1)
    entry = jnp.where(z == 0, jnp.zeros_like(entry), entry)
    for d in range(1, G):
        from_mate(d).wait_recv()
    a1 = a128[i] * a128[i]
    total = b_ref[G - 1].astype(F32)
    power = a1
    for k in range(G - 2, -1, -1):
        total = total + same(ends[k], ends[G - 1]) * power * b_ref[k].astype(F32)
        power = power * a1
    x_ref[...] = total.astype(BF16)

    def to_plane(d):
        return remote(x_ref, xr.at[d], x_send.at[d], x_recv.at[d], (p + G * d) % n)

    for d in range(1, planes):
        @pl.when(z + d < planes)
        def _():
            to_plane(d).start()

    pairs(cuts[1], cuts[2], local)

    a1 = a128[i] * a128[i]
    a4 = a1 * a1
    a4 = a4 * a4
    lead = jnp.ones_like(a4)
    for d in range(1, planes):
        lead = jnp.where(z >= d, lead * a4, lead)
    acc[...] = same(entry, jnp.zeros_like(entry)) * lead * carry_ref[:, lanes(i, wq)]
    power = jnp.ones_like(a4)
    for d in range(1, planes):
        @pl.when(z >= d)
        def _():
            to_plane(d).wait_recv()
            acc[...] += same(end_of(G * (z - d) + G - 1), entry) * power * xr[d].astype(F32)
        power = power * a4
    state = acc[...]
    s3[0] = state.astype(BF16)
    power = a1
    for k in range(1, G):
        held = same(ends[k - 1], entry) * power * state
        power = power * a1
        fall = None
        for b in range(k - 1, -1, -1):
            term = same(ends[b], ends[k - 1]) * b_ref[b].astype(F32)
            held = held + (term if fall is None else term * fall)
            fall = a1 if fall is None else fall * a1
        s3[k] = held.astype(BF16)

    def back(d):
        k = (i + d) % G
        return remote(s3.at[k], sin.at[i], s3_send.at[d], s3_recv.at[i], z * G + k)

    def back_from(d):
        k = (i + d) % G
        return remote(s3.at[k], sin.at[k], s3_send.at[d], s3_recv.at[k], z * G + k)

    for d in range(1, G):
        back(d).start()
    sin[i] = s3[i]

    pairs(cuts[2], cuts[3], local)

    for d in range(1, G):
        back_from(d).wait_recv()

    def emit(t):
        return pltpu.make_async_copy(outb.at[:, lanes(t)], out_hbm.at[:, lanes(t)], osem.at[t])

    def finish(t):
        at = lanes(t)
        state = sin[t // per, :, lanes(t % per)]
        later = keep_ref[0:1, 0:1] * a128[t // per, :, lanes(t % per)] * state.astype(F32) + s0_ref[:, at]
        for j, held in enumerate((state, later.astype(BF16))):
            rows = slice(j * L, (j + 1) * L)
            cross = mm(cw[rows, at], spread(held, diag16_ref[...]))
            outb[rows, at] = (q_ref[rows, at] * (part[rows, at] + cross)).astype(BF16)
        emit(t).start()

    pairs(0, tiles, lambda t, slot: finish(t))

    @pl.when(p < n - 1)
    def _():
        tail_copy.wait_send()
    for d in range(1, G):
        to_mate(d).wait_send()
        back(d).wait_send()
    for d in range(1, planes):
        @pl.when(z + d < planes)
        def _():
            to_plane(d).wait_send()
    lax.fori_loop(0, tiles, lambda t, c: (emit(t).wait(), c)[1], 0)


def body(features, short_weight, residues, rates, skip, carry_state, earlier_rows, segment_ids):
    count, _, width = features.shape
    groups, modes = rates.shape
    tiles = width // W
    wq = width // G
    n = lax.axis_size("ctx")
    planes = n // G
    vmem = pl.BlockSpec(memory_space=pltpu.VMEM)
    hbm = pl.BlockSpec(memory_space=pl.ANY)
    dma = pltpu.SemaphoreType.DMA
    return pl.pallas_call(
        functools.partial(kernel, n),
        in_specs=[vmem, hbm, vmem, vmem, vmem, vmem, vmem, vmem],
        out_specs=hbm,
        out_shape=jax.ShapeDtypeStruct((count, width), BF16),
        scratch_shapes=[
            pltpu.VMEM((3, count, width), BF16),
            pltpu.VMEM((3, 16, width), BF16),
            pltpu.VMEM((16, width // 2), BF16),
            pltpu.VMEM((16, width // 2), BF16),
            pltpu.VMEM((3, 8, width), F32),
            pltpu.VMEM((count, L), BF16),
            pltpu.VMEM((2, count, L), F32),
            pltpu.VMEM((count, L), F32),
            pltpu.VMEM((8, L), F32),
            pltpu.VMEM((W, W), F32),
            pltpu.VMEM((W, W), BF16),
            pltpu.VMEM((16, L), F32),
            pltpu.VMEM((2, groups * modes, L), BF16),
            pltpu.VMEM((count, groups * modes), BF16),
            pltpu.VMEM((groups, L), F32),
            pltpu.VMEM((G, modes, wq), F32),
            pltpu.VMEM((count, width), BF16),
            pltpu.VMEM((count, width), F32),
            pltpu.VMEM((count, width), F32),
            pltpu.VMEM((modes, width), F32),
            pltpu.VMEM((G, modes, wq), BF16),
            pltpu.VMEM((G, modes, wq), BF16),
            pltpu.VMEM((modes, wq), BF16),
            pltpu.VMEM((planes, modes, wq), BF16),
            pltpu.VMEM((modes, wq), F32),
            pltpu.VMEM((G, modes, wq), BF16),
            pltpu.VMEM((G, modes, wq), BF16),
            pltpu.VMEM((2, 2, L, GT * L), BF16),
            pltpu.VMEM((2, 2, GT * L, W), BF16),
            pltpu.VMEM((count, width), BF16),
            dma((width // FW,)),
            dma, dma, dma,
            dma((G,)), dma((G,)),
            dma((planes,)), dma((planes,)),
            dma((G,)), dma((G,)),
            dma((tiles,)),
        ],
        compiler_params=pltpu.CompilerParams(
            collective_id=0, has_side_effects=True, vmem_limit_bytes=56 * 1024 * 1024),
        name="hyena",
    )(segment_ids.reshape(-1, L), features.transpose(1, 0, 2), earlier_rows.transpose(1, 0, 2), short_weight,
      skip.reshape(1, -1), rates.T, residues.T, carry_state)


def solution(mesh):
    placed = (
        P(("groups", "ctx"), None, None),
        P(),
        P(),
        P(),
        P(),
        P("groups", None),
        P("groups", None, None),
        P("groups"),
    )
    return jax.shard_map(
        body, mesh=mesh, in_specs=placed, out_specs=P(("groups", "ctx"), None), check_vma=False
    )
```

```python
import functools

import jax
import jax.numpy as jnp
from jax import lax
from jax.experimental import pallas as pl
from jax.experimental.pallas import tpu as pltpu
from jax.sharding import PartitionSpec as P

F32 = jnp.float32
BF16 = jnp.bfloat16
L = 128
W = 128
MODES = 16
FG = 16
GT = W // FG
G = 4
FW = 512
SLOTS = 4
PARTS = 8


def column(row):
    return jnp.transpose(jnp.broadcast_to(row, (row.shape[1], row.shape[1])))


def segment_tables(seg_ref, block, mask_ref, near_ref, cmask_ref, dmask_ref):
    rows = [seg_ref[pl.ds(2 * block + j, 1), :] for j in range(2)]
    before = seg_ref[pl.ds(jnp.maximum(2 * block - 1, 0), 1), :]
    before = jnp.where(block == 0, jnp.zeros_like(before), before)
    lane = lax.broadcasted_iota(jnp.int32, (1, L), 1)
    t_at = lax.broadcasted_iota(jnp.int32, (L, L), 0)
    s_at = lax.broadcasted_iota(jnp.int32, (L, L), 1)
    for j in range(2):
        row = rows[j]
        last = before if j == 0 else rows[0]
        one, two = last[:, L - 1 : L], last[:, L - 2 : L - 1]
        prev1 = jnp.where(lane == 0, one, pltpu.roll(row, 1, 1))
        prev2 = jnp.where(lane == 0, two, jnp.where(lane == 1, one, pltpu.roll(row, 2, 1)))
        near_ref[0, j * L : (j + 1) * L, :] = column((prev1 == row).astype(F32))
        near_ref[1, j * L : (j + 1) * L, :] = column((prev2 == row).astype(F32))
        cmask_ref[j * L : (j + 1) * L, :] = column((row == one).astype(F32))
        dmask_ref[j : j + 1, :] = (row == row[:, L - 1 : L]).astype(F32)
        seg_t = column(row.astype(F32))
        keep = (seg_t == row.astype(F32)) & (t_at >= s_at)
        mask_ref[j * L : (j + 1) * L, :] = keep.astype(F32).astype(BF16)
    keep0 = (rows[0][:, L - 1 : L] == before[:, L - 1 : L]).astype(F32)
    keep1 = (rows[1][:, L - 1 : L] == rows[0][:, L - 1 : L]).astype(F32)
    return keep0, keep1


def block_diagonal():
    r = lax.broadcasted_iota(jnp.int32, (W, W), 0) // FG
    c = lax.broadcasted_iota(jnp.int32, (W, W), 1) // FG
    return (r == c).astype(F32)


def wide(mask):
    return jnp.concatenate([mask] * (W // L), axis=1)


def short_filter(x, prev, taps, near_ref):
    row = lax.broadcasted_iota(jnp.int32, (8, W), 0)
    x1 = pltpu.roll(x, 1, 0)
    x2 = pltpu.roll(x, 2, 0)
    h1 = jnp.where(row == 0, prev[1:2], x1[:8])
    h2 = jnp.where(row == 0, prev[0:1], jnp.where(row == 1, prev[1:2], x2[:8]))
    x1 = jnp.concatenate([h1, x1[8:]], axis=0)
    x2 = jnp.concatenate([h2, x2[8:]], axis=0)
    return taps[0:1] * x + wide(near_ref[0]) * (taps[1:2] * x1) + wide(near_ref[1]) * (taps[2:3] * x2)


def end_decay(rate_col):
    lag = (L - 1) - lax.broadcasted_iota(jnp.int32, (W, L), 1)
    return jnp.exp(-rate_col * lag.astype(F32))


def fold(full, diag):
    return jnp.sum((full * diag).reshape(GT, MODES, W), axis=0)


def spread(state, diag16):
    return jnp.concatenate([state] * GT, axis=0) * diag16


def mm(a, b):
    return lax.dot_general(a, b, (((1,), (0,)), ((), ())), preferred_element_type=F32)


def kernel(n, seg_ref, feat_hbm, earlier_ref, taps_ref, skip_ref, rate_ref, res_ref, carry_ref, out_hbm,
           feat, tail16, pack, got, prev, mask_ref, near_ref, cmask_ref, dmask_ref, diag_ref, diag16_ref, keep_ref,
           dec, cw, hs, a128, u_ref, q_ref, part, s0_ref, sumq, b_ref, x_ref, xr, acc, s3, sin, big, val, outb,
           fsem, tsem, tail_send, tail_recv, s1_send, s1_recv, x_send, x_recv, s3_send, s3_recv, osem):
    count, width = u_ref.shape
    tiles = width // W
    wq = width // G
    per = wq // W
    planes = n // G
    p = lax.axis_index("ctx")
    i, z = p % G, p // G

    def lanes(t, size=W):
        return pl.ds(pl.multiple_of(t * size, size), size)

    def fetch(t):
        return pltpu.make_async_copy(feat_hbm.at[:, :, lanes(t, FW)], feat.at[:, :, lanes(t, FW)], fsem.at[t])

    def remote(src, dst, send, recv, target):
        return pltpu.make_async_remote_copy(
            src_ref=src, dst_ref=dst, send_sem=send, recv_sem=recv,
            device_id={"ctx": target}, device_id_type=pl.DeviceIdType.MESH,
        )

    barrier = pltpu.get_barrier_semaphore()

    def greet(d, c):
        pl.semaphore_signal(barrier, inc=1, device_id={"ctx": (p + d) % n}, device_id_type=pl.DeviceIdType.MESH)
        return c

    lax.fori_loop(1, n, greet, 0)
    rows16 = pltpu.make_async_copy(feat_hbm.at[:, pl.ds(count - 16, 16), :], tail16, tsem)
    rows16.start()
    lax.fori_loop(0, width // FW, lambda t, c: (fetch(t).start(), c)[1], 0)

    keep0, keep1 = segment_tables(seg_ref, p, mask_ref, near_ref, cmask_ref, dmask_ref)
    keep_ref[0:8, :] = jnp.broadcast_to(keep0, (8, L))
    keep_ref[8:16, :] = jnp.broadcast_to(keep1, (8, L))
    diag = block_diagonal()
    diag_ref[...] = diag
    diag16_ref[...] = diag.astype(BF16)

    half = width // 2
    rows16.wait()
    pieces = []
    for a in range(3):
        last = tail16[a].astype(F32)[14:16]
        pieces += [last[:, :half], last[:, half:]]
    pack[...] = jnp.concatenate(pieces + [jnp.zeros((4, half), F32)], axis=0).astype(BF16)
    weight_mg = res_ref[...] * jnp.sqrt(rate_ref[...])

    def tables(t):
        back = (rate_ref.shape[1] - GT * t) % rate_ref.shape[1]
        rates = pltpu.roll(rate_ref[...], back, 1)
        weights = pltpu.roll(weight_mg, back, 1)
        spell = lambda v: jnp.concatenate(
            [jnp.broadcast_to(v[:, g : g + 1], (MODES, L)) for g in range(GT)], axis=0)
        rate_col, weight_col = spell(rates), spell(weights)
        decay = end_decay(rate_col)
        rows = lanes(t)
        for j in range(2):
            dec[j, rows, :] = (decay * dmask_ref[j : j + 1]).astype(BF16)
        table = jnp.sum((weight_col * decay).reshape(GT, MODES, L), axis=1)
        hs[lanes(t, GT), :] = pltpu.roll(table, 1, 1)
        step = lax.broadcasted_iota(jnp.int32, (W, L), 1) + 1
        cross = jnp.transpose(weight_col * jnp.exp(-rate_col * step.astype(F32)))
        for j in range(2):
            cw[j * L : (j + 1) * L, rows] = (cross * wide(cmask_ref[j * L : (j + 1) * L, :])).astype(BF16)
        a128[t // per, :, lanes(t % per)] = jnp.exp(-L * fold(wide(rate_col), diag_ref[...]))

    def pairs(begin, end, step):
        def group(r, c):
            for slot in range(SLOTS):
                step(SLOTS * r + slot, slot)
            return c
        lax.fori_loop(begin // SLOTS, end // SLOTS, group, 0)

    first = tiles // 2 // SLOTS * SLOTS
    pairs(0, first, lambda t, slot: tables(t))
    pl.semaphore_wait(barrier, n - 1)
    tail_copy = remote(pack, got, tail_send, tail_recv, (p + 1) % n)

    @pl.when(p < n - 1)
    def _():
        tail_copy.start()

    pairs(first, tiles, lambda t, slot: tables(t))

    @pl.when(p == 0)
    def _():
        for a in range(3):
            prev[a, 0:2, :] = earlier_ref[a].astype(F32)

    @pl.when(p > 0)
    def _():
        tail_copy.wait_recv()
        rows = got[...].astype(F32)
        for a in range(3):
            for h in range(2):
                prev[a, 0:2, h * half : (h + 1) * half] = rows[4 * a + 2 * h : 4 * a + 2 * h + 2]

    lax.fori_loop(0, width // FW, lambda t, c: (fetch(t).wait(), c)[1], 0)

    def filtered(a, at):
        return short_filter(feat[a, :, at].astype(F32), prev[a, 0:2, at], taps_ref[:, a, at], near_ref)

    def sums(t):
        at = lanes(t)
        u = (filtered(1, at) * filtered(2, at)).astype(BF16)
        u_ref[:, at] = u
        both = [fold(mm(dec[j, at, :], u[j * L : (j + 1) * L]), diag_ref[...]) for j in range(2)]
        s0_ref[:, at] = both[0]
        total = keep_ref[8:9, 0:1] * a128[t // per, :, lanes(t % per)] * both[0] + both[1]
        sumq[t // per, :, lanes(t % per)] = total.astype(BF16)

    pairs(0, tiles, lambda t, slot: sums(t))

    def to_mate(d):
        k = (i + d) % G
        return remote(sumq.at[k], b_ref.at[i], s1_send.at[d], s1_recv.at[i], z * G + k)

    def from_mate(d):
        k = (i + d) % G
        return remote(sumq.at[k], b_ref.at[k], s1_send.at[d], s1_recv.at[k], z * G + k)

    for d in range(1, G):
        to_mate(d).start()
    b_ref[i] = sumq[i]

    def local(t, slot):
        at = lanes(t)
        u = u_ref[:, at]
        table = hs[lanes(t, GT), :]
        for g in range(GT):
            square = jnp.broadcast_to(table[g : g + 1], (L, L))
            square = pltpu.roll(square, 0, 1, stride=1, stride_axis=0).astype(BF16)
            own = jnp.concatenate([diag16_ref[g * FG : (g + 1) * FG, :]] * (L // FG), axis=0)
            for j in range(2):
                big[slot, j, :, g * L : (g + 1) * L] = square * mask_ref[j * L : (j + 1) * L, :]
                val[slot, j, g * L : (g + 1) * L, :] = u[j * L : (j + 1) * L] * own
        for j in range(2):
            part[j * L : (j + 1) * L, at] = (
                mm(big[slot, j], val[slot, j]) + skip_ref[:, at] * u[j * L : (j + 1) * L].astype(F32))
        q_ref[:, at] = filtered(0, at)

    cuts = [0, tiles // 4 // SLOTS * SLOTS, 3 * tiles // 4 // SLOTS * SLOTS, tiles]
    pairs(cuts[0], cuts[1], local)

    def end_of(block):
        return seg_ref[pl.ds(jnp.maximum(2 * block + 1, 0), 1), L - 1 : L]

    def same(one, two):
        return (one == two).astype(F32)

    ends = [end_of(z * G + k) for k in range(G)]
    entry = end_of(z * G - 1)
    entry = jnp.where(z == 0, jnp.zeros_like(entry), entry)
    for d in range(1, G):
        from_mate(d).wait_recv()
    a1 = a128[i] * a128[i]
    total = b_ref[G - 1].astype(F32)
    power = a1
    for k in range(G - 2, -1, -1):
        total = total + same(ends[k], ends[G - 1]) * power * b_ref[k].astype(F32)
        power = power * a1
    x_ref[...] = total.astype(BF16)

    def to_plane(d):
        return remote(x_ref, xr.at[d], x_send.at[d], x_recv.at[d], (p + G * d) % n)

    for d in range(1, planes):
        @pl.when(z + d < planes)
        def _():
            to_plane(d).start()

    pairs(cuts[1], cuts[2], local)

    a1 = a128[i] * a128[i]
    a4 = a1 * a1
    a4 = a4 * a4
    lead = jnp.ones_like(a4)
    for d in range(1, planes):
        lead = jnp.where(z >= d, lead * a4, lead)
    acc[...] = same(entry, jnp.zeros_like(entry)) * lead * carry_ref[:, lanes(i, wq)]
    power = jnp.ones_like(a4)
    for d in range(1, planes):
        @pl.when(z >= d)
        def _():
            to_plane(d).wait_recv()
            acc[...] += same(end_of(G * (z - d) + G - 1), entry) * power * xr[d].astype(F32)
        power = power * a4
    state = acc[...]
    s3[0] = state.astype(BF16)
    power = a1
    for k in range(1, G):
        held = same(ends[k - 1], entry) * power * state
        power = power * a1
        fall = None
        for b in range(k - 1, -1, -1):
            term = same(ends[b], ends[k - 1]) * b_ref[b].astype(F32)
            held = held + (term if fall is None else term * fall)
            fall = a1 if fall is None else fall * a1
        s3[k] = held.astype(BF16)

    def back(d):
        k = (i + d) % G
        return remote(s3.at[k], sin.at[i], s3_send.at[d], s3_recv.at[i], z * G + k)

    def back_from(d):
        k = (i + d) % G
        return remote(s3.at[k], sin.at[k], s3_send.at[d], s3_recv.at[k], z * G + k)

    for d in range(1, G):
        back(d).start()
    sin[i] = s3[i]

    pairs(cuts[2], cuts[3], local)

    for d in range(1, G):
        back_from(d).wait_recv()

    def emit(t):
        return pltpu.make_async_copy(outb.at[:, lanes(t)], out_hbm.at[:, lanes(t)], osem.at[t])

    def finish(t):
        at = lanes(t)
        state = sin[t // per, :, lanes(t % per)]
        later = keep_ref[0:1, 0:1] * a128[t // per, :, lanes(t % per)] * state.astype(F32) + s0_ref[:, at]
        for j, held in enumerate((state, later.astype(BF16))):
            rows = slice(j * L, (j + 1) * L)
            cross = mm(cw[rows, at], spread(held, diag16_ref[...]))
            outb[rows, at] = (q_ref[rows, at] * (part[rows, at] + cross)).astype(BF16)
        emit(t).start()

    pairs(0, tiles, lambda t, slot: finish(t))

    @pl.when(p < n - 1)
    def _():
        tail_copy.wait_send()
    for d in range(1, G):
        to_mate(d).wait_send()
        back(d).wait_send()
    for d in range(1, planes):
        @pl.when(z + d < planes)
        def _():
            to_plane(d).wait_send()
    lax.fori_loop(0, tiles, lambda t, c: (emit(t).wait(), c)[1], 0)


def hand_over(in_ref, out_ref, sem):
    rows = in_ref.shape[0] // PARTS
    copies = [
        pltpu.make_async_copy(in_ref.at[pl.ds(k * rows, rows)], out_ref.at[pl.ds(k * rows, rows)], sem.at[k])
        for k in range(PARTS)
    ]
    for copy in copies:
        copy.start()
    for copy in copies:
        copy.wait()


def body(features, short_weight, residues, rates, skip, carry_state, earlier_rows, segment_ids):
    count, _, width = features.shape
    groups, modes = rates.shape
    tiles = width // W
    wq = width // G
    n = lax.axis_size("ctx")
    planes = n // G
    vmem = pl.BlockSpec(memory_space=pltpu.VMEM)
    hbm = pl.BlockSpec(memory_space=pl.ANY)
    dma = pltpu.SemaphoreType.DMA
    mixed = pl.pallas_call(
        functools.partial(kernel, n),
        in_specs=[vmem, hbm, vmem, vmem, vmem, vmem, vmem, vmem],
        out_specs=hbm,
        out_shape=jax.ShapeDtypeStruct((count, width), BF16),
        scratch_shapes=[
            pltpu.VMEM((3, count, width), BF16),
            pltpu.VMEM((3, 16, width), BF16),
            pltpu.VMEM((16, width // 2), BF16),
            pltpu.VMEM((16, width // 2), BF16),
            pltpu.VMEM((3, 8, width), F32),
            pltpu.VMEM((count, L), BF16),
            pltpu.VMEM((2, count, L), F32),
            pltpu.VMEM((count, L), F32),
            pltpu.VMEM((8, L), F32),
            pltpu.VMEM((W, W), F32),
            pltpu.VMEM((W, W), BF16),
            pltpu.VMEM((16, L), F32),
            pltpu.VMEM((2, groups * modes, L), BF16),
            pltpu.VMEM((count, groups * modes), BF16),
            pltpu.VMEM((groups, L), F32),
            pltpu.VMEM((G, modes, wq), F32),
            pltpu.VMEM((count, width), BF16),
            pltpu.VMEM((count, width), F32),
            pltpu.VMEM((count, width), F32),
            pltpu.VMEM((modes, width), F32),
            pltpu.VMEM((G, modes, wq), BF16),
            pltpu.VMEM((G, modes, wq), BF16),
            pltpu.VMEM((modes, wq), BF16),
            pltpu.VMEM((planes, modes, wq), BF16),
            pltpu.VMEM((modes, wq), F32),
            pltpu.VMEM((G, modes, wq), BF16),
            pltpu.VMEM((G, modes, wq), BF16),
            pltpu.VMEM((SLOTS, 2, L, GT * L), BF16),
            pltpu.VMEM((SLOTS, 2, GT * L, W), BF16),
            pltpu.VMEM((count, width), BF16),
            dma((width // FW,)),
            dma, dma, dma,
            dma((G,)), dma((G,)),
            dma((planes,)), dma((planes,)),
            dma((G,)), dma((G,)),
            dma((tiles,)),
        ],
        compiler_params=pltpu.CompilerParams(
            collective_id=0, has_side_effects=True, vmem_limit_bytes=56 * 1024 * 1024),
        name="hyena",
    )(segment_ids.reshape(-1, L), features.transpose(1, 0, 2), earlier_rows.transpose(1, 0, 2), short_weight,
      skip.reshape(1, -1), rates.T, residues.T, carry_state)
    return pl.pallas_call(
        hand_over,
        in_specs=[hbm],
        out_specs=hbm,
        out_shape=jax.ShapeDtypeStruct((count, width), BF16),
        scratch_shapes=[dma((PARTS,))],
        compiler_params=pltpu.CompilerParams(vmem_limit_bytes=56 * 1024 * 1024),
        name="hand_over",
    )(mixed)


def solution(mesh):
    placed = (
        P(("groups", "ctx"), None, None),
        P(),
        P(),
        P(),
        P(),
        P("groups", None),
        P("groups", None, None),
        P("groups"),
    )
    return jax.shard_map(
        body, mesh=mesh, in_specs=placed, out_specs=P(("groups", "ctx"), None), check_vma=False
    )
```

```python
import functools

import jax
import jax.numpy as jnp
from jax import lax
from jax.experimental import pallas as pl
from jax.experimental.pallas import tpu as pltpu
from jax.sharding import PartitionSpec as P

F32 = jnp.float32
BF16 = jnp.bfloat16
HS = BF16
L = 128
W = 256
MODES = 16
FG = 16
GT = W // FG
G = 4
FW = 512
GW = 512


def column(row):
    return jnp.transpose(jnp.broadcast_to(row, (row.shape[1], row.shape[1])))


def segment_tables(seg_ref, block, mask_ref, near_ref, cmask_ref, dmask_ref):
    rows = [seg_ref[pl.ds(2 * block + j, 1), :] for j in range(2)]
    before = seg_ref[pl.ds(jnp.maximum(2 * block - 1, 0), 1), :]
    before = jnp.where(block == 0, jnp.zeros_like(before), before)
    lane = lax.broadcasted_iota(jnp.int32, (1, L), 1)
    t_at = lax.broadcasted_iota(jnp.int32, (L, L), 0)
    s_at = lax.broadcasted_iota(jnp.int32, (L, L), 1)
    for j in range(2):
        row = rows[j]
        last = before if j == 0 else rows[0]
        one, two = last[:, L - 1 : L], last[:, L - 2 : L - 1]
        prev1 = jnp.where(lane == 0, one, pltpu.roll(row, 1, 1))
        prev2 = jnp.where(lane == 0, two, jnp.where(lane == 1, one, pltpu.roll(row, 2, 1)))
        near_ref[0, j * L : (j + 1) * L, :] = column((prev1 == row).astype(F32))
        near_ref[1, j * L : (j + 1) * L, :] = column((prev2 == row).astype(F32))
        cmask_ref[j * L : (j + 1) * L, :] = column((row == one).astype(F32))
        dmask_ref[j : j + 1, :] = (row == row[:, L - 1 : L]).astype(F32)
        seg_t = column(row.astype(F32))
        keep = (seg_t == row.astype(F32)) & (t_at >= s_at)
        mask_ref[j * L : (j + 1) * L, :] = keep.astype(F32).astype(BF16)
    keep0 = (rows[0][:, L - 1 : L] == before[:, L - 1 : L]).astype(F32)
    keep1 = (rows[1][:, L - 1 : L] == rows[0][:, L - 1 : L]).astype(F32)
    return keep0, keep1


def block_diagonal():
    r = lax.broadcasted_iota(jnp.int32, (W, W), 0) // FG
    c = lax.broadcasted_iota(jnp.int32, (W, W), 1) // FG
    return (r == c).astype(F32)


def wide(mask):
    return jnp.concatenate([mask, mask], axis=1)


def short_filter(x, prev, taps, near_ref):
    row = lax.broadcasted_iota(jnp.int32, (8, W), 0)
    x1 = pltpu.roll(x, 1, 0)
    x2 = pltpu.roll(x, 2, 0)
    h1 = jnp.where(row == 0, prev[1:2], x1[:8])
    h2 = jnp.where(row == 0, prev[0:1], jnp.where(row == 1, prev[1:2], x2[:8]))
    x1 = jnp.concatenate([h1, x1[8:]], axis=0)
    x2 = jnp.concatenate([h2, x2[8:]], axis=0)
    return taps[0:1] * x + wide(near_ref[0]) * (taps[1:2] * x1) + wide(near_ref[1]) * (taps[2:3] * x2)


def end_decay(rate_col):
    lag = (L - 1) - lax.broadcasted_iota(jnp.int32, (W, L), 1)
    return jnp.exp(-rate_col * lag.astype(F32))


def fold(full, diag):
    return jnp.sum((full * diag).reshape(GT, MODES, W), axis=0)


def spread(state, diag16):
    return jnp.concatenate([state] * GT, axis=0) * diag16


def mm(a, b):
    return lax.dot_general(a, b, (((1,), (0,)), ((), ())), preferred_element_type=F32)


def kernel(n, seg_ref, feat_hbm, earlier_ref, taps_ref, skip_ref, rate_ref, res_ref, carry_ref, out_hbm, first_ref,
           feat, tail16, pack, got, prev, mask_ref, near_ref, cmask_ref, dmask_ref, diag_ref, diag16_ref, keep_ref,
           dec, cw, hs, a128, u_ref, part, s0_ref, sumq, b_ref, x_ref, xr, acc, s3, sin, big, val, outb,
           fsem, tsem, tail_send, tail_recv, s1_send, s1_recv, x_send, x_recv, s3_send, s3_recv, osem):
    count, width = u_ref.shape
    tiles = width // W
    wq = width // G
    per = wq // W
    planes = n // G
    p = lax.axis_index("ctx")
    i, z = p % G, p // G

    def lanes(t, size=W):
        return pl.ds(pl.multiple_of(t * size, size), size)

    def fetch(t):
        return pltpu.make_async_copy(feat_hbm.at[:, :, lanes(t, FW)], feat.at[:, :, lanes(t, FW)], fsem.at[t])

    def remote(src, dst, send, recv, target):
        return pltpu.make_async_remote_copy(
            src_ref=src, dst_ref=dst, send_sem=send, recv_sem=recv,
            device_id={"ctx": target}, device_id_type=pl.DeviceIdType.MESH,
        )

    barrier = pltpu.get_barrier_semaphore()

    def greet(d, c):
        pl.semaphore_signal(barrier, inc=1, device_id={"ctx": (p + d) % n}, device_id_type=pl.DeviceIdType.MESH)
        return c

    lax.fori_loop(1, n, greet, 0)
    rows16 = pltpu.make_async_copy(feat_hbm.at[:, pl.ds(count - 16, 16), :], tail16, tsem)
    rows16.start()
    lax.fori_loop(0, width // FW, lambda t, c: (fetch(t).start(), c)[1], 0)

    keep0, keep1 = segment_tables(seg_ref, p, mask_ref, near_ref, cmask_ref, dmask_ref)
    keep_ref[0:8, :] = jnp.broadcast_to(keep0, (8, L))
    keep_ref[8:16, :] = jnp.broadcast_to(keep1, (8, L))
    diag = block_diagonal()
    diag_ref[...] = diag
    diag16_ref[...] = diag.astype(BF16)

    half = width // 2
    rows16.wait()
    pieces = []
    for a in range(3):
        last = tail16[a].astype(F32)[14:16]
        pieces += [last[:, :half], last[:, half:]]
    pack[...] = jnp.concatenate(pieces + [jnp.zeros((4, half), F32)], axis=0).astype(BF16)
    val[...] = jnp.zeros_like(val)

    weight_mg = res_ref[...] * jnp.sqrt(rate_ref[...])

    def tables(t):
        back = (rate_ref.shape[1] - GT * t) % rate_ref.shape[1]
        rates = pltpu.roll(rate_ref[...], back, 1)
        weights = pltpu.roll(weight_mg, back, 1)
        spell = lambda v: jnp.concatenate(
            [jnp.broadcast_to(v[:, g : g + 1], (MODES, L)) for g in range(GT)], axis=0)
        rate_col, weight_col = spell(rates), spell(weights)
        decay = end_decay(rate_col)
        rows = lanes(t)
        for j in range(2):
            dec[j, rows, :] = (decay * dmask_ref[j : j + 1]).astype(BF16)
        table = jnp.sum((weight_col * decay).reshape(GT, MODES, L), axis=1)
        table = pltpu.roll(table, 1, 1)
        base = [
            pltpu.roll(jnp.broadcast_to(table[g : g + 1], (FG, L)), 0, 1, stride=1, stride_axis=0) for g in range(GT)
        ]
        hs[rows, :] = jnp.concatenate(base, axis=0).astype(hs.dtype)
        step = lax.broadcasted_iota(jnp.int32, (W, L), 1) + 1
        cross = jnp.transpose(weight_col * jnp.exp(-rate_col * step.astype(F32)))
        for j in range(2):
            cw[j * L : (j + 1) * L, rows] = (cross * wide(cmask_ref[j * L : (j + 1) * L, :])).astype(BF16)
        a128[t // per, :, lanes(t % per)] = jnp.exp(-L * fold(wide(rate_col), diag_ref[...]))

    def pairs(begin, end, step):
        def both(t2, c):
            step(2 * t2, 0)
            step(2 * t2 + 1, 1)
            return c
        lax.fori_loop(begin // 2, end // 2, both, 0)

    first = tiles // 2 // 2 * 2
    pairs(0, first, lambda t, slot: tables(t))
    pl.semaphore_wait(barrier, n - 1)
    tail_copy = remote(pack, got, tail_send, tail_recv, (p + 1) % n)

    @pl.when(p < n - 1)
    def _():
        tail_copy.start()

    pairs(first, tiles, lambda t, slot: tables(t))

    @pl.when(p == 0)
    def _():
        for a in range(3):
            prev[a, 0:2, :] = earlier_ref[a].astype(F32)

    @pl.when(p > 0)
    def _():
        tail_copy.wait_recv()
        rows = got[...].astype(F32)
        for a in range(3):
            for h in range(2):
                prev[a, 0:2, h * half : (h + 1) * half] = rows[4 * a + 2 * h : 4 * a + 2 * h + 2]

    first_ref[...] = prev[0]
    lax.fori_loop(0, width // FW, lambda t, c: (fetch(t).wait(), c)[1], 0)

    def filtered(a, at):
        return short_filter(feat[a, :, at].astype(F32), prev[a, 0:2, at], taps_ref[:, a, at], near_ref)

    def sums(t):
        at = lanes(t)
        u = (filtered(1, at) * filtered(2, at)).astype(BF16)
        u_ref[:, at] = u
        both = [fold(mm(dec[j, at, :], u[j * L : (j + 1) * L]), diag_ref[...]) for j in range(2)]
        s0_ref[:, at] = both[0]
        total = keep_ref[8:9, 0:1] * a128[t // per, :, lanes(t % per)] * both[0] + both[1]
        sumq[t // per, :, lanes(t % per)] = total.astype(BF16)

    pairs(0, tiles, lambda t, slot: sums(t))

    def to_mate(d):
        k = (i + d) % G
        return remote(sumq.at[k], b_ref.at[i], s1_send.at[d], s1_recv.at[i], z * G + k)

    def from_mate(d):
        k = (i + d) % G
        return remote(sumq.at[k], b_ref.at[k], s1_send.at[d], s1_recv.at[k], z * G + k)

    for d in range(1, G):
        to_mate(d).start()
    b_ref[i] = sumq[i]

    def local(t, slot):
        at = lanes(t)
        u = u_ref[:, at]
        for g in range(GT):
            base = hs[pl.ds(pl.multiple_of(t * W + g * FG, FG), FG), :]
            square = jnp.concatenate(
                [base] + [pltpu.roll(base, FG * k, 1) for k in range(1, L // FG)], axis=0).astype(BF16)
            side = g * FG // L * L
            own = diag16_ref[g * FG : (g + 1) * FG, side : side + L]
            own = jnp.concatenate([own] * (L // FG), axis=0)
            for j in range(2):
                big[slot, j, :, g * L : (g + 1) * L] = square * mask_ref[j * L : (j + 1) * L, :]
                val[slot, j, g * L : (g + 1) * L, side : side + L] = (
                    u[j * L : (j + 1) * L, side : side + L] * own)
        for j in range(2):
            part[j * L : (j + 1) * L, at] = (
                mm(big[slot, j], val[slot, j]) + skip_ref[:, at] * u[j * L : (j + 1) * L].astype(F32))

    cuts = [0, tiles // 4 // 2 * 2, 3 * tiles // 4 // 2 * 2, tiles]
    pairs(cuts[0], cuts[1], local)

    def end_of(block):
        return seg_ref[pl.ds(jnp.maximum(2 * block + 1, 0), 1), L - 1 : L]

    def same(one, two):
        return (one == two).astype(F32)

    ends = [end_of(z * G + k) for k in range(G)]
    entry = end_of(z * G - 1)
    entry = jnp.where(z == 0, jnp.zeros_like(entry), entry)
    for d in range(1, G):
        from_mate(d).wait_recv()
    a1 = a128[i] * a128[i]
    total = b_ref[G - 1].astype(F32)
    power = a1
    for k in range(G - 2, -1, -1):
        total = total + same(ends[k], ends[G - 1]) * power * b_ref[k].astype(F32)
        power = power * a1
    x_ref[...] = total.astype(BF16)

    def to_plane(d):
        return remote(x_ref, xr.at[d], x_send.at[d], x_recv.at[d], (p + G * d) % n)

    for d in range(1, planes):
        @pl.when(z + d < planes)
        def _():
            to_plane(d).start()

    pairs(cuts[1], cuts[2], local)

    a1 = a128[i] * a128[i]
    a4 = a1 * a1
    a4 = a4 * a4
    lead = jnp.ones_like(a4)
    for d in range(1, planes):
        lead = jnp.where(z >= d, lead * a4, lead)
    acc[...] = same(entry, jnp.zeros_like(entry)) * lead * carry_ref[:, lanes(i, wq)]
    power = jnp.ones_like(a4)
    for d in range(1, planes):
        @pl.when(z >= d)
        def _():
            to_plane(d).wait_recv()
            acc[...] += same(end_of(G * (z - d) + G - 1), entry) * power * xr[d].astype(F32)
        power = power * a4
    state = acc[...]
    s3[0] = state.astype(BF16)
    power = a1
    for k in range(1, G):
        held = same(ends[k - 1], entry) * power * state
        power = power * a1
        fall = None
        for b in range(k - 1, -1, -1):
            term = same(ends[b], ends[k - 1]) * b_ref[b].astype(F32)
            held = held + (term if fall is None else term * fall)
            fall = a1 if fall is None else fall * a1
        s3[k] = held.astype(BF16)

    def back(d):
        k = (i + d) % G
        return remote(s3.at[k], sin.at[i], s3_send.at[d], s3_recv.at[i], z * G + k)

    def back_from(d):
        k = (i + d) % G
        return remote(s3.at[k], sin.at[k], s3_send.at[d], s3_recv.at[k], z * G + k)

    for d in range(1, G):
        back(d).start()
    sin[i] = s3[i]

    pairs(cuts[2], cuts[3], local)

    for d in range(1, G):
        back_from(d).wait_recv()

    def emit(t):
        return pltpu.make_async_copy(outb.at[:, lanes(t)], out_hbm.at[:, lanes(t)], osem.at[t])

    def finish(t):
        at = lanes(t)
        state = sin[t // per, :, lanes(t % per)]
        later = keep_ref[0:1, 0:1] * a128[t // per, :, lanes(t % per)] * state.astype(F32) + s0_ref[:, at]
        for j, held in enumerate((state, later.astype(BF16))):
            rows = slice(j * L, (j + 1) * L)
            cross = mm(cw[rows, at], spread(held, diag16_ref[...]))
            outb[rows, at] = (part[rows, at] + cross).astype(BF16)
        emit(t).start()

    pairs(0, tiles, lambda t, slot: finish(t))

    @pl.when(p < n - 1)
    def _():
        tail_copy.wait_send()
    for d in range(1, G):
        to_mate(d).wait_send()
        back(d).wait_send()
    for d in range(1, planes):
        @pl.when(z + d < planes)
        def _():
            to_plane(d).wait_send()
    lax.fori_loop(0, tiles, lambda t, c: (emit(t).wait(), c)[1], 0)


def gate_kernel(seg_ref, feat_ref, first_ref, taps_ref, total_ref, out_ref, mask_ref, near_ref, cmask_ref, dmask_ref):
    @pl.when(pl.program_id(0) == 0)
    def _():
        segment_tables(seg_ref, lax.axis_index("ctx"), mask_ref, near_ref, cmask_ref, dmask_ref)

    for c in range(GW // W):
        at = slice(c * W, (c + 1) * W)
        q = short_filter(feat_ref[0, :, at].astype(F32), first_ref[0:2, at], taps_ref[:, 0, at], near_ref)
        out_ref[:, at] = (q * total_ref[:, at].astype(F32)).astype(BF16)


def body(features, short_weight, residues, rates, skip, carry_state, earlier_rows, segment_ids):
    count, _, width = features.shape
    groups, modes = rates.shape
    tiles = width // W
    wq = width // G
    n = lax.axis_size("ctx")
    planes = n // G
    vmem = pl.BlockSpec(memory_space=pltpu.VMEM)
    hbm = pl.BlockSpec(memory_space=pl.ANY)
    dma = pltpu.SemaphoreType.DMA
    seg = segment_ids.reshape(-1, L)
    feat = features.transpose(1, 0, 2)
    total, first = pl.pallas_call(
        functools.partial(kernel, n),
        in_specs=[vmem, hbm, vmem, vmem, vmem, vmem, vmem, vmem],
        out_specs=[hbm, vmem],
        out_shape=[jax.ShapeDtypeStruct((count, width), BF16), jax.ShapeDtypeStruct((8, width), F32)],
        scratch_shapes=[
            pltpu.VMEM((3, count, width), BF16),
            pltpu.VMEM((3, 16, width), BF16),
            pltpu.VMEM((16, width // 2), BF16),
            pltpu.VMEM((16, width // 2), BF16),
            pltpu.VMEM((3, 8, width), F32),
            pltpu.VMEM((count, L), BF16),
            pltpu.VMEM((2, count, L), F32),
            pltpu.VMEM((count, L), F32),
            pltpu.VMEM((8, L), F32),
            pltpu.VMEM((W, W), F32),
            pltpu.VMEM((W, W), BF16),
            pltpu.VMEM((16, L), F32),
            pltpu.VMEM((2, groups * modes, L), BF16),
            pltpu.VMEM((count, groups * modes), BF16),
            pltpu.VMEM((groups * FG, L), HS),
            pltpu.VMEM((G, modes, wq), F32),
            pltpu.VMEM((count, width), BF16),
            pltpu.VMEM((count, width), F32),
            pltpu.VMEM((modes, width), F32),
            pltpu.VMEM((G, modes, wq), BF16),
            pltpu.VMEM((G, modes, wq), BF16),
            pltpu.VMEM((modes, wq), BF16),
            pltpu.VMEM((planes, modes, wq), BF16),
            pltpu.VMEM((modes, wq), F32),
            pltpu.VMEM((G, modes, wq), BF16),
            pltpu.VMEM((G, modes, wq), BF16),
            pltpu.VMEM((2, 2, L, GT * L), BF16),
            pltpu.VMEM((2, 2, GT * L, W), BF16),
            pltpu.VMEM((count, width), BF16),
            dma((width // FW,)),
            dma, dma, dma,
            dma((G,)), dma((G,)),
            dma((planes,)), dma((planes,)),
            dma((G,)), dma((G,)),
            dma((tiles,)),
        ],
        compiler_params=pltpu.CompilerParams(
            collective_id=0, has_side_effects=True, vmem_limit_bytes=56 * 1024 * 1024),
        name="hyena",
    )(seg, feat, earlier_rows.transpose(1, 0, 2), short_weight,
      skip.reshape(1, -1), rates.T, residues.T, carry_state)
    whole = lambda shape: pl.BlockSpec(shape, lambda i: (0,) * len(shape))
    return pl.pallas_call(
        gate_kernel,
        grid=(width // GW,),
        in_specs=[
            whole(seg.shape),
            pl.BlockSpec((1, count, GW), lambda i: (0, 0, i)),
            pl.BlockSpec((8, GW), lambda i: (0, i)),
            pl.BlockSpec((3, 3, GW), lambda i: (0, 0, i)),
            pl.BlockSpec((count, GW), lambda i: (0, i)),
        ],
        out_specs=pl.BlockSpec((count, GW), lambda i: (0, i)),
        out_shape=jax.ShapeDtypeStruct((count, width), BF16),
        scratch_shapes=[
            pltpu.VMEM((count, L), BF16),
            pltpu.VMEM((2, count, L), F32),
            pltpu.VMEM((count, L), F32),
            pltpu.VMEM((8, L), F32),
        ],
        compiler_params=pltpu.CompilerParams(vmem_limit_bytes=56 * 1024 * 1024),
        name="gate",
    )(seg, feat, first, short_weight, total)


def solution(mesh):
    placed = (
        P(("groups", "ctx"), None, None),
        P(),
        P(),
        P(),
        P(),
        P("groups", None),
        P("groups", None, None),
        P("groups"),
    )
    return jax.shard_map(
        body, mesh=mesh, in_specs=placed, out_specs=P(("groups", "ctx"), None), check_vma=False
    )
```

```python
import functools

import jax
import jax.numpy as jnp
from jax import lax
from jax.experimental import pallas as pl
from jax.experimental.pallas import tpu as pltpu
from jax.sharding import PartitionSpec as P

F32 = jnp.float32
BF16 = jnp.bfloat16
HS = BF16
L = 128
W = 256
MODES = 16
FG = 16
GT = W // FG
G = 4
FW = 512
GW = 512


def column(row):
    return jnp.transpose(jnp.broadcast_to(row, (row.shape[1], row.shape[1])))


def segment_tables(seg_ref, block, mask_ref, near_ref, cmask_ref, dmask_ref):
    rows = [seg_ref[pl.ds(2 * block + j, 1), :] for j in range(2)]
    before = seg_ref[pl.ds(jnp.maximum(2 * block - 1, 0), 1), :]
    before = jnp.where(block == 0, jnp.zeros_like(before), before)
    lane = lax.broadcasted_iota(jnp.int32, (1, L), 1)
    t_at = lax.broadcasted_iota(jnp.int32, (L, L), 0)
    s_at = lax.broadcasted_iota(jnp.int32, (L, L), 1)
    for j in range(2):
        row = rows[j]
        last = before if j == 0 else rows[0]
        one, two = last[:, L - 1 : L], last[:, L - 2 : L - 1]
        prev1 = jnp.where(lane == 0, one, pltpu.roll(row, 1, 1))
        prev2 = jnp.where(lane == 0, two, jnp.where(lane == 1, one, pltpu.roll(row, 2, 1)))
        near_ref[0, j * L : (j + 1) * L, :] = column((prev1 == row).astype(F32))
        near_ref[1, j * L : (j + 1) * L, :] = column((prev2 == row).astype(F32))
        cmask_ref[j * L : (j + 1) * L, :] = column((row == one).astype(F32))
        dmask_ref[j : j + 1, :] = (row == row[:, L - 1 : L]).astype(F32)
        seg_t = column(row.astype(F32))
        keep = (seg_t == row.astype(F32)) & (t_at >= s_at)
        mask_ref[j * L : (j + 1) * L, :] = keep.astype(F32).astype(BF16)
    keep0 = (rows[0][:, L - 1 : L] == before[:, L - 1 : L]).astype(F32)
    keep1 = (rows[1][:, L - 1 : L] == rows[0][:, L - 1 : L]).astype(F32)
    return keep0, keep1


def block_diagonal():
    r = lax.broadcasted_iota(jnp.int32, (W, W), 0) // FG
    c = lax.broadcasted_iota(jnp.int32, (W, W), 1) // FG
    return (r == c).astype(F32)


def wide(mask):
    return jnp.concatenate([mask, mask], axis=1)


def shift_tables(near_ref, shift_ref):
    count = near_ref.shape[1]
    t_at = lax.broadcasted_iota(jnp.int32, (count, L), 0)
    s_at = lax.broadcasted_iota(jnp.int32, (count, L), 1)
    for k in range(2):
        for c in range(count // L):
            pick = jnp.where(t_at - (k + 1) == s_at + c * L, near_ref[k], 0.0)
            shift_ref[k * count : (k + 1) * count, c * L : (c + 1) * L] = pick.astype(BF16)


def short_filter(x, prev, taps, near_ref, shift_ref):
    count, size = x.shape
    moved = mm(shift_ref[...], x)
    y = taps[0:1] * x.astype(F32) + taps[1:2] * moved[:count] + taps[2:3] * moved[count:]
    row = lax.broadcasted_iota(jnp.int32, (8, size), 0)
    one, two = [jnp.concatenate([near_ref[k, 0:8, :]] * (size // L), axis=1) for k in range(2)]
    at0 = one * (taps[1:2] * prev[1:2]) + two * (taps[2:3] * prev[0:1])
    at1 = two * (taps[2:3] * prev[1:2])
    fix = jnp.where(row == 0, at0, jnp.where(row == 1, at1, 0.0))
    return jnp.concatenate([y[:8] + fix, y[8:]], axis=0)


def end_decay(rate_col):
    lag = (L - 1) - lax.broadcasted_iota(jnp.int32, (W, L), 1)
    return jnp.exp(-rate_col * lag.astype(F32))


def fold(full, diag):
    return jnp.sum((full * diag).reshape(GT, MODES, W), axis=0)


def spread(state, diag16):
    return jnp.concatenate([state] * GT, axis=0) * diag16


def mm(a, b):
    return lax.dot_general(a, b, (((1,), (0,)), ((), ())), preferred_element_type=F32)


def kernel(n, seg_ref, feat_hbm, earlier_ref, taps_ref, skip_ref, rate_ref, res_ref, carry_ref, out_hbm, first_ref,
           feat, tail16, pack, got, prev, mask_ref, near_ref, cmask_ref, dmask_ref, shift_ref, diag_ref, diag16_ref, keep_ref,
           dec, cw, hs, a128, u_ref, part, s0_ref, sumq, b_ref, x_ref, xr, acc, s3, sin, big, val, outb,
           fsem, tsem, tail_send, tail_recv, s1_send, s1_recv, x_send, x_recv, s3_send, s3_recv, osem):
    count, width = u_ref.shape
    tiles = width // W
    wq = width // G
    per = wq // W
    planes = n // G
    p = lax.axis_index("ctx")
    i, z = p % G, p // G

    def lanes(t, size=W):
        return pl.ds(pl.multiple_of(t * size, size), size)

    def fetch(t):
        return pltpu.make_async_copy(feat_hbm.at[:, :, lanes(t, FW)], feat.at[:, :, lanes(t, FW)], fsem.at[t])

    def remote(src, dst, send, recv, target):
        return pltpu.make_async_remote_copy(
            src_ref=src, dst_ref=dst, send_sem=send, recv_sem=recv,
            device_id={"ctx": target}, device_id_type=pl.DeviceIdType.MESH,
        )

    barrier = pltpu.get_barrier_semaphore()

    def greet(d, c):
        pl.semaphore_signal(barrier, inc=1, device_id={"ctx": (p + d) % n}, device_id_type=pl.DeviceIdType.MESH)
        return c

    lax.fori_loop(1, n, greet, 0)
    rows16 = pltpu.make_async_copy(feat_hbm.at[:, pl.ds(count - 16, 16), :], tail16, tsem)
    rows16.start()
    lax.fori_loop(0, width // FW, lambda t, c: (fetch(t).start(), c)[1], 0)

    keep0, keep1 = segment_tables(seg_ref, p, mask_ref, near_ref, cmask_ref, dmask_ref)
    shift_tables(near_ref, shift_ref)
    keep_ref[0:8, :] = jnp.broadcast_to(keep0, (8, L))
    keep_ref[8:16, :] = jnp.broadcast_to(keep1, (8, L))
    diag = block_diagonal()
    diag_ref[...] = diag
    diag16_ref[...] = diag.astype(BF16)

    half = width // 2
    rows16.wait()
    pieces = []
    for a in range(3):
        last = tail16[a].astype(F32)[14:16]
        pieces += [last[:, :half], last[:, half:]]
    pack[...] = jnp.concatenate(pieces + [jnp.zeros((4, half), F32)], axis=0).astype(BF16)
    val[...] = jnp.zeros_like(val)

    weight_mg = res_ref[...] * jnp.sqrt(rate_ref[...])

    def tables(t):
        back = (rate_ref.shape[1] - GT * t) % rate_ref.shape[1]
        rates = pltpu.roll(rate_ref[...], back, 1)
        weights = pltpu.roll(weight_mg, back, 1)
        spell = lambda v: jnp.concatenate(
            [jnp.broadcast_to(v[:, g : g + 1], (MODES, L)) for g in range(GT)], axis=0)
        rate_col, weight_col = spell(rates), spell(weights)
        decay = end_decay(rate_col)
        rows = lanes(t)
        for j in range(2):
            dec[j, rows, :] = (decay * dmask_ref[j : j + 1]).astype(BF16)
        table = jnp.sum((weight_col * decay).reshape(GT, MODES, L), axis=1)
        table = pltpu.roll(table, 1, 1)
        base = [
            pltpu.roll(jnp.broadcast_to(table[g : g + 1], (FG, L)), 0, 1, stride=1, stride_axis=0) for g in range(GT)
        ]
        hs[rows, :] = jnp.concatenate(base, axis=0).astype(hs.dtype)
        step = lax.broadcasted_iota(jnp.int32, (W, L), 1) + 1
        cross = jnp.transpose(weight_col * jnp.exp(-rate_col * step.astype(F32)))
        for j in range(2):
            cw[j * L : (j + 1) * L, rows] = (cross * wide(cmask_ref[j * L : (j + 1) * L, :])).astype(BF16)
        a128[t // per, :, lanes(t % per)] = jnp.exp(-L * fold(wide(rate_col), diag_ref[...]))

    def pairs(begin, end, step):
        def both(t2, c):
            step(2 * t2, 0)
            step(2 * t2 + 1, 1)
            return c
        lax.fori_loop(begin // 2, end // 2, both, 0)

    first = tiles // 2 // 2 * 2
    pairs(0, first, lambda t, slot: tables(t))
    pl.semaphore_wait(barrier, n - 1)
    tail_copy = remote(pack, got, tail_send, tail_recv, (p + 1) % n)

    @pl.when(p < n - 1)
    def _():
        tail_copy.start()

    pairs(first, tiles, lambda t, slot: tables(t))

    @pl.when(p == 0)
    def _():
        for a in range(3):
            prev[a, 0:2, :] = earlier_ref[a].astype(F32)

    @pl.when(p > 0)
    def _():
        tail_copy.wait_recv()
        rows = got[...].astype(F32)
        for a in range(3):
            for h in range(2):
                prev[a, 0:2, h * half : (h + 1) * half] = rows[4 * a + 2 * h : 4 * a + 2 * h + 2]

    first_ref[...] = prev[0]
    lax.fori_loop(0, width // FW, lambda t, c: (fetch(t).wait(), c)[1], 0)

    def filtered(a, at):
        return short_filter(feat[a, :, at], prev[a, 0:2, at], taps_ref[:, a, at], near_ref, shift_ref)

    def sums(t):
        at = lanes(t)
        u = (filtered(1, at) * filtered(2, at)).astype(BF16)
        u_ref[:, at] = u
        both = [fold(mm(dec[j, at, :], u[j * L : (j + 1) * L]), diag_ref[...]) for j in range(2)]
        s0_ref[:, at] = both[0]
        total = keep_ref[8:9, 0:1] * a128[t // per, :, lanes(t % per)] * both[0] + both[1]
        sumq[t // per, :, lanes(t % per)] = total.astype(BF16)

    pairs(0, tiles, lambda t, slot: sums(t))

    def to_mate(d):
        k = (i + d) % G
        return remote(sumq.at[k], b_ref.at[i], s1_send.at[d], s1_recv.at[i], z * G + k)

    def from_mate(d):
        k = (i + d) % G
        return remote(sumq.at[k], b_ref.at[k], s1_send.at[d], s1_recv.at[k], z * G + k)

    for d in range(1, G):
        to_mate(d).start()
    b_ref[i] = sumq[i]

    def local(t, slot):
        at = lanes(t)
        u = u_ref[:, at]
        for g in range(GT):
            base = hs[pl.ds(pl.multiple_of(t * W + g * FG, FG), FG), :]
            square = jnp.concatenate(
                [base] + [pltpu.roll(base, FG * k, 1) for k in range(1, L // FG)], axis=0).astype(BF16)
            side = g * FG // L * L
            own = diag16_ref[g * FG : (g + 1) * FG, side : side + L]
            own = jnp.concatenate([own] * (L // FG), axis=0)
            for j in range(2):
                big[slot, j, :, g * L : (g + 1) * L] = square * mask_ref[j * L : (j + 1) * L, :]
                val[slot, j, g * L : (g + 1) * L, side : side + L] = (
                    u[j * L : (j + 1) * L, side : side + L] * own)
        for j in range(2):
            part[j * L : (j + 1) * L, at] = (
                mm(big[slot, j], val[slot, j]) + skip_ref[:, at] * u[j * L : (j + 1) * L].astype(F32))

    cuts = [0, tiles // 4 // 2 * 2, 3 * tiles // 4 // 2 * 2, tiles]
    pairs(cuts[0], cuts[1], local)

    def end_of(block):
        return seg_ref[pl.ds(jnp.maximum(2 * block + 1, 0), 1), L - 1 : L]

    def same(one, two):
        return (one == two).astype(F32)

    ends = [end_of(z * G + k) for k in range(G)]
    entry = end_of(z * G - 1)
    entry = jnp.where(z == 0, jnp.zeros_like(entry), entry)
    for d in range(1, G):
        from_mate(d).wait_recv()
    a1 = a128[i] * a128[i]
    total = b_ref[G - 1].astype(F32)
    power = a1
    for k in range(G - 2, -1, -1):
        total = total + same(ends[k], ends[G - 1]) * power * b_ref[k].astype(F32)
        power = power * a1
    x_ref[...] = total.astype(BF16)

    def to_plane(d):
        return remote(x_ref, xr.at[d], x_send.at[d], x_recv.at[d], (p + G * d) % n)

    for d in range(1, planes):
        @pl.when(z + d < planes)
        def _():
            to_plane(d).start()

    pairs(cuts[1], cuts[2], local)

    a1 = a128[i] * a128[i]
    a4 = a1 * a1
    a4 = a4 * a4
    lead = jnp.ones_like(a4)
    for d in range(1, planes):
        lead = jnp.where(z >= d, lead * a4, lead)
    acc[...] = same(entry, jnp.zeros_like(entry)) * lead * carry_ref[:, lanes(i, wq)]
    power = jnp.ones_like(a4)
    for d in range(1, planes):
        @pl.when(z >= d)
        def _():
            to_plane(d).wait_recv()
            acc[...] += same(end_of(G * (z - d) + G - 1), entry) * power * xr[d].astype(F32)
        power = power * a4
    state = acc[...]
    s3[0] = state.astype(BF16)
    power = a1
    for k in range(1, G):
        held = same(ends[k - 1], entry) * power * state
        power = power * a1
        fall = None
        for b in range(k - 1, -1, -1):
            term = same(ends[b], ends[k - 1]) * b_ref[b].astype(F32)
            held = held + (term if fall is None else term * fall)
            fall = a1 if fall is None else fall * a1
        s3[k] = held.astype(BF16)

    def back(d):
        k = (i + d) % G
        return remote(s3.at[k], sin.at[i], s3_send.at[d], s3_recv.at[i], z * G + k)

    def back_from(d):
        k = (i + d) % G
        return remote(s3.at[k], sin.at[k], s3_send.at[d], s3_recv.at[k], z * G + k)

    for d in range(1, G):
        back(d).start()
    sin[i] = s3[i]

    pairs(cuts[2], cuts[3], local)

    for d in range(1, G):
        back_from(d).wait_recv()

    def emit(t):
        return pltpu.make_async_copy(outb.at[:, lanes(t)], out_hbm.at[:, lanes(t)], osem.at[t])

    def finish(t):
        at = lanes(t)
        state = sin[t // per, :, lanes(t % per)]
        later = keep_ref[0:1, 0:1] * a128[t // per, :, lanes(t % per)] * state.astype(F32) + s0_ref[:, at]
        for j, held in enumerate((state, later.astype(BF16))):
            rows = slice(j * L, (j + 1) * L)
            cross = mm(cw[rows, at], spread(held, diag16_ref[...]))
            outb[rows, at] = (part[rows, at] + cross).astype(BF16)
        emit(t).start()

    pairs(0, tiles, lambda t, slot: finish(t))

    @pl.when(p < n - 1)
    def _():
        tail_copy.wait_send()
    for d in range(1, G):
        to_mate(d).wait_send()
        back(d).wait_send()
    for d in range(1, planes):
        @pl.when(z + d < planes)
        def _():
            to_plane(d).wait_send()
    lax.fori_loop(0, tiles, lambda t, c: (emit(t).wait(), c)[1], 0)


def gate_kernel(seg_ref, feat_ref, first_ref, taps_ref, total_ref, out_ref, mask_ref, near_ref, cmask_ref, dmask_ref,
                shift_ref):
    @pl.when(pl.program_id(0) == 0)
    def _():
        segment_tables(seg_ref, lax.axis_index("ctx"), mask_ref, near_ref, cmask_ref, dmask_ref)
        shift_tables(near_ref, shift_ref)

    for c in range(GW // W):
        at = slice(c * W, (c + 1) * W)
        q = short_filter(feat_ref[0, :, at], first_ref[0:2, at], taps_ref[:, 0, at], near_ref, shift_ref)
        out_ref[:, at] = (q * total_ref[:, at].astype(F32)).astype(BF16)


def body(features, short_weight, residues, rates, skip, carry_state, earlier_rows, segment_ids):
    count, _, width = features.shape
    groups, modes = rates.shape
    tiles = width // W
    wq = width // G
    n = lax.axis_size("ctx")
    planes = n // G
    vmem = pl.BlockSpec(memory_space=pltpu.VMEM)
    hbm = pl.BlockSpec(memory_space=pl.ANY)
    dma = pltpu.SemaphoreType.DMA
    seg = segment_ids.reshape(-1, L)
    feat = features.transpose(1, 0, 2)
    total, first = pl.pallas_call(
        functools.partial(kernel, n),
        in_specs=[vmem, hbm, vmem, vmem, vmem, vmem, vmem, vmem],
        out_specs=[hbm, vmem],
        out_shape=[jax.ShapeDtypeStruct((count, width), BF16), jax.ShapeDtypeStruct((8, width), F32)],
        scratch_shapes=[
            pltpu.VMEM((3, count, width), BF16),
            pltpu.VMEM((3, 16, width), BF16),
            pltpu.VMEM((16, width // 2), BF16),
            pltpu.VMEM((16, width // 2), BF16),
            pltpu.VMEM((3, 8, width), F32),
            pltpu.VMEM((count, L), BF16),
            pltpu.VMEM((2, count, L), F32),
            pltpu.VMEM((count, L), F32),
            pltpu.VMEM((8, L), F32),
            pltpu.VMEM((2 * count, count), BF16),
            pltpu.VMEM((W, W), F32),
            pltpu.VMEM((W, W), BF16),
            pltpu.VMEM((16, L), F32),
            pltpu.VMEM((2, groups * modes, L), BF16),
            pltpu.VMEM((count, groups * modes), BF16),
            pltpu.VMEM((groups * FG, L), HS),
            pltpu.VMEM((G, modes, wq), F32),
            pltpu.VMEM((count, width), BF16),
            pltpu.VMEM((count, width), F32),
            pltpu.VMEM((modes, width), F32),
            pltpu.VMEM((G, modes, wq), BF16),
            pltpu.VMEM((G, modes, wq), BF16),
            pltpu.VMEM((modes, wq), BF16),
            pltpu.VMEM((planes, modes, wq), BF16),
            pltpu.VMEM((modes, wq), F32),
            pltpu.VMEM((G, modes, wq), BF16),
            pltpu.VMEM((G, modes, wq), BF16),
            pltpu.VMEM((2, 2, L, GT * L), BF16),
            pltpu.VMEM((2, 2, GT * L, W), BF16),
            pltpu.VMEM((count, width), BF16),
            dma((width // FW,)),
            dma, dma, dma,
            dma((G,)), dma((G,)),
            dma((planes,)), dma((planes,)),
            dma((G,)), dma((G,)),
            dma((tiles,)),
        ],
        compiler_params=pltpu.CompilerParams(
            collective_id=0, has_side_effects=True, vmem_limit_bytes=56 * 1024 * 1024),
        name="hyena",
    )(seg, feat, earlier_rows.transpose(1, 0, 2), short_weight,
      skip.reshape(1, -1), rates.T, residues.T, carry_state)
    whole = lambda shape: pl.BlockSpec(shape, lambda i: (0,) * len(shape))
    return pl.pallas_call(
        gate_kernel,
        grid=(width // GW,),
        in_specs=[
            whole(seg.shape),
            pl.BlockSpec((1, count, GW), lambda i: (0, 0, i)),
            pl.BlockSpec((8, GW), lambda i: (0, i)),
            pl.BlockSpec((3, 3, GW), lambda i: (0, 0, i)),
            pl.BlockSpec((count, GW), lambda i: (0, i)),
        ],
        out_specs=pl.BlockSpec((count, GW), lambda i: (0, i)),
        out_shape=jax.ShapeDtypeStruct((count, width), BF16),
        scratch_shapes=[
            pltpu.VMEM((count, L), BF16),
            pltpu.VMEM((2, count, L), F32),
            pltpu.VMEM((count, L), F32),
            pltpu.VMEM((8, L), F32),
            pltpu.VMEM((2 * count, count), BF16),
        ],
        compiler_params=pltpu.CompilerParams(vmem_limit_bytes=56 * 1024 * 1024),
        name="gate",
    )(seg, feat, first, short_weight, total)


def solution(mesh):
    placed = (
        P(("groups", "ctx"), None, None),
        P(),
        P(),
        P(),
        P(),
        P("groups", None),
        P("groups", None, None),
        P("groups"),
    )
    return jax.shard_map(
        body, mesh=mesh, in_specs=placed, out_specs=P(("groups", "ctx"), None), check_vma=False
    )
```

```python
import functools

import jax
import jax.numpy as jnp
from jax import lax
from jax.experimental import pallas as pl
from jax.experimental.pallas import tpu as pltpu
from jax.sharding import PartitionSpec as P

F32 = jnp.float32
BF16 = jnp.bfloat16
HS = BF16
L = 128
W = 256
MODES = 16
FG = 16
GT = W // FG
G = 4
FW = 512
GW = 2048


def column(row):
    return jnp.transpose(jnp.broadcast_to(row, (row.shape[1], row.shape[1])))


def segment_tables(seg_ref, block, mask_ref, near_ref, cmask_ref, dmask_ref):
    rows = [seg_ref[pl.ds(2 * block + j, 1), :] for j in range(2)]
    before = seg_ref[pl.ds(jnp.maximum(2 * block - 1, 0), 1), :]
    before = jnp.where(block == 0, jnp.zeros_like(before), before)
    lane = lax.broadcasted_iota(jnp.int32, (1, L), 1)
    t_at = lax.broadcasted_iota(jnp.int32, (L, L), 0)
    s_at = lax.broadcasted_iota(jnp.int32, (L, L), 1)
    for j in range(2):
        row = rows[j]
        last = before if j == 0 else rows[0]
        one, two = last[:, L - 1 : L], last[:, L - 2 : L - 1]
        prev1 = jnp.where(lane == 0, one, pltpu.roll(row, 1, 1))
        prev2 = jnp.where(lane == 0, two, jnp.where(lane == 1, one, pltpu.roll(row, 2, 1)))
        near_ref[0, j * L : (j + 1) * L, :] = column((prev1 == row).astype(F32))
        near_ref[1, j * L : (j + 1) * L, :] = column((prev2 == row).astype(F32))
        cmask_ref[j * L : (j + 1) * L, :] = column((row == one).astype(F32))
        dmask_ref[j : j + 1, :] = (row == row[:, L - 1 : L]).astype(F32)
        seg_t = column(row.astype(F32))
        keep = (seg_t == row.astype(F32)) & (t_at >= s_at)
        mask_ref[j * L : (j + 1) * L, :] = keep.astype(F32).astype(BF16)
    keep0 = (rows[0][:, L - 1 : L] == before[:, L - 1 : L]).astype(F32)
    keep1 = (rows[1][:, L - 1 : L] == rows[0][:, L - 1 : L]).astype(F32)
    return keep0, keep1


def block_diagonal():
    r = lax.broadcasted_iota(jnp.int32, (W, W), 0) // FG
    c = lax.broadcasted_iota(jnp.int32, (W, W), 1) // FG
    return (r == c).astype(F32)


def wide(mask):
    return jnp.concatenate([mask, mask], axis=1)


def short_filter(x, prev, taps, near_ref):
    row = lax.broadcasted_iota(jnp.int32, (8, W), 0)
    x1 = pltpu.roll(x, 1, 0)
    x2 = pltpu.roll(x, 2, 0)
    h1 = jnp.where(row == 0, prev[1:2], x1[:8])
    h2 = jnp.where(row == 0, prev[0:1], jnp.where(row == 1, prev[1:2], x2[:8]))
    x1 = jnp.concatenate([h1, x1[8:]], axis=0)
    x2 = jnp.concatenate([h2, x2[8:]], axis=0)
    return taps[0:1] * x + wide(near_ref[0]) * (taps[1:2] * x1) + wide(near_ref[1]) * (taps[2:3] * x2)


def end_decay(rate_col):
    lag = (L - 1) - lax.broadcasted_iota(jnp.int32, (W, L), 1)
    return jnp.exp(-rate_col * lag.astype(F32))


def fold(full, diag):
    return jnp.sum((full * diag).reshape(GT, MODES, W), axis=0)


def spread(state, diag16):
    return jnp.concatenate([state] * GT, axis=0) * diag16


def mm(a, b):
    return lax.dot_general(a, b, (((1,), (0,)), ((), ())), preferred_element_type=F32)


def kernel(n, seg_ref, feat_hbm, earlier_ref, taps_ref, skip_ref, rate_ref, res_ref, carry_ref, out_hbm, first_ref,
           feat, tail16, pack, got, prev, mask_ref, near_ref, cmask_ref, dmask_ref, diag_ref, diag16_ref, keep_ref,
           dec, cw, hs, a128, u_ref, part, s0_ref, sumq, b_ref, x_ref, xr, acc, s3, sin, big, val, outb,
           fsem, tsem, tail_send, tail_recv, s1_send, s1_recv, x_send, x_recv, s3_send, s3_recv, osem):
    count, width = u_ref.shape
    tiles = width // W
    wq = width // G
    per = wq // W
    planes = n // G
    p = lax.axis_index("ctx")
    i, z = p % G, p // G

    def lanes(t, size=W):
        return pl.ds(pl.multiple_of(t * size, size), size)

    def fetch(t):
        return pltpu.make_async_copy(
            feat_hbm.at[pl.ds(1, 2), :, lanes(t, FW)], feat.at[pl.ds(1, 2), :, lanes(t, FW)], fsem.at[t])

    def remote(src, dst, send, recv, target):
        return pltpu.make_async_remote_copy(
            src_ref=src, dst_ref=dst, send_sem=send, recv_sem=recv,
            device_id={"ctx": target}, device_id_type=pl.DeviceIdType.MESH,
        )

    barrier = pltpu.get_barrier_semaphore()

    def greet(d, c):
        pl.semaphore_signal(barrier, inc=1, device_id={"ctx": (p + d) % n}, device_id_type=pl.DeviceIdType.MESH)
        return c

    lax.fori_loop(1, n, greet, 0)
    rows16 = pltpu.make_async_copy(feat_hbm.at[:, pl.ds(count - 16, 16), :], tail16, tsem)
    rows16.start()
    lax.fori_loop(0, width // FW, lambda t, c: (fetch(t).start(), c)[1], 0)

    keep0, keep1 = segment_tables(seg_ref, p, mask_ref, near_ref, cmask_ref, dmask_ref)
    keep_ref[0:8, :] = jnp.broadcast_to(keep0, (8, L))
    keep_ref[8:16, :] = jnp.broadcast_to(keep1, (8, L))
    diag = block_diagonal()
    diag_ref[...] = diag
    diag16_ref[...] = diag.astype(BF16)

    half = width // 2
    rows16.wait()
    pieces = []
    for a in range(3):
        last = tail16[a].astype(F32)[14:16]
        pieces += [last[:, :half], last[:, half:]]
    pack[...] = jnp.concatenate(pieces + [jnp.zeros((4, half), F32)], axis=0).astype(BF16)
    val[...] = jnp.zeros_like(val)

    weight_mg = res_ref[...] * jnp.sqrt(rate_ref[...])

    def tables(t):
        back = (rate_ref.shape[1] - GT * t) % rate_ref.shape[1]
        rates = pltpu.roll(rate_ref[...], back, 1)
        weights = pltpu.roll(weight_mg, back, 1)
        spell = lambda v: jnp.concatenate(
            [jnp.broadcast_to(v[:, g : g + 1], (MODES, L)) for g in range(GT)], axis=0)
        rate_col, weight_col = spell(rates), spell(weights)
        decay = end_decay(rate_col)
        rows = lanes(t)
        for j in range(2):
            dec[j, rows, :] = (decay * dmask_ref[j : j + 1]).astype(BF16)
        table = jnp.sum((weight_col * decay).reshape(GT, MODES, L), axis=1)
        table = pltpu.roll(table, 1, 1)
        base = [
            pltpu.roll(jnp.broadcast_to(table[g : g + 1], (FG, L)), 0, 1, stride=1, stride_axis=0) for g in range(GT)
        ]
        hs[rows, :] = jnp.concatenate(base, axis=0).astype(hs.dtype)
        step = lax.broadcasted_iota(jnp.int32, (W, L), 1) + 1
        cross = jnp.transpose(weight_col * jnp.exp(-rate_col * step.astype(F32)))
        for j in range(2):
            cw[j * L : (j + 1) * L, rows] = (cross * wide(cmask_ref[j * L : (j + 1) * L, :])).astype(BF16)
        a128[t // per, :, lanes(t % per)] = jnp.exp(-L * fold(wide(rate_col), diag_ref[...]))

    def pairs(begin, end, step):
        def both(t2, c):
            step(2 * t2, 0)
            step(2 * t2 + 1, 1)
            return c
        lax.fori_loop(begin // 2, end // 2, both, 0)

    first = tiles // 2 // 2 * 2
    pairs(0, first, lambda t, slot: tables(t))
    pl.semaphore_wait(barrier, n - 1)
    tail_copy = remote(pack, got, tail_send, tail_recv, (p + 1) % n)

    @pl.when(p < n - 1)
    def _():
        tail_copy.start()

    pairs(first, tiles, lambda t, slot: tables(t))

    @pl.when(p == 0)
    def _():
        for a in range(3):
            prev[a, 0:2, :] = earlier_ref[a].astype(F32)

    @pl.when(p > 0)
    def _():
        tail_copy.wait_recv()
        rows = got[...].astype(F32)
        for a in range(3):
            for h in range(2):
                prev[a, 0:2, h * half : (h + 1) * half] = rows[4 * a + 2 * h : 4 * a + 2 * h + 2]

    first_ref[...] = prev[0]

    def filtered(a, at):
        return short_filter(feat[a, :, at].astype(F32), prev[a, 0:2, at], taps_ref[:, a, at], near_ref)

    def sums(t):
        at = lanes(t)
        u = (filtered(1, at) * filtered(2, at)).astype(BF16)
        u_ref[:, at] = u
        both = [fold(mm(dec[j, at, :], u[j * L : (j + 1) * L]), diag_ref[...]) for j in range(2)]
        s0_ref[:, at] = both[0]
        total = keep_ref[8:9, 0:1] * a128[t // per, :, lanes(t % per)] * both[0] + both[1]
        sumq[t // per, :, lanes(t % per)] = total.astype(BF16)

    def fetched_sums(t, slot):
        if slot == 0:
            fetch(t * W // FW).wait()
        sums(t)

    pairs(0, tiles, fetched_sums)

    def to_mate(d):
        k = (i + d) % G
        return remote(sumq.at[k], b_ref.at[i], s1_send.at[d], s1_recv.at[i], z * G + k)

    def from_mate(d):
        k = (i + d) % G
        return remote(sumq.at[k], b_ref.at[k], s1_send.at[d], s1_recv.at[k], z * G + k)

    for d in range(1, G):
        to_mate(d).start()
    b_ref[i] = sumq[i]

    def local(t, slot):
        at = lanes(t)
        u = u_ref[:, at]
        for g in range(GT):
            base = hs[pl.ds(pl.multiple_of(t * W + g * FG, FG), FG), :]
            square = jnp.concatenate(
                [base] + [pltpu.roll(base, FG * k, 1) for k in range(1, L // FG)], axis=0).astype(BF16)
            side = g * FG // L * L
            own = diag16_ref[g * FG : (g + 1) * FG, side : side + L]
            own = jnp.concatenate([own] * (L // FG), axis=0)
            for j in range(2):
                big[slot, j, :, g * L : (g + 1) * L] = square * mask_ref[j * L : (j + 1) * L, :]
                val[slot, j, g * L : (g + 1) * L, side : side + L] = (
                    u[j * L : (j + 1) * L, side : side + L] * own)
        for j in range(2):
            part[j * L : (j + 1) * L, at] = (
                mm(big[slot, j], val[slot, j]) + skip_ref[:, at] * u[j * L : (j + 1) * L].astype(F32))

    cuts = [0, tiles // 4 // 2 * 2, 3 * tiles // 4 // 2 * 2, tiles]
    pairs(cuts[0], cuts[1], local)

    def end_of(block):
        return seg_ref[pl.ds(jnp.maximum(2 * block + 1, 0), 1), L - 1 : L]

    def same(one, two):
        return (one == two).astype(F32)

    ends = [end_of(z * G + k) for k in range(G)]
    entry = end_of(z * G - 1)
    entry = jnp.where(z == 0, jnp.zeros_like(entry), entry)
    for d in range(1, G):
        from_mate(d).wait_recv()
    a1 = a128[i] * a128[i]
    total = b_ref[G - 1].astype(F32)
    power = a1
    for k in range(G - 2, -1, -1):
        total = total + same(ends[k], ends[G - 1]) * power * b_ref[k].astype(F32)
        power = power * a1
    x_ref[...] = total.astype(BF16)

    def to_plane(d):
        return remote(x_ref, xr.at[d], x_send.at[d], x_recv.at[d], (p + G * d) % n)

    for d in range(1, planes):
        @pl.when(z + d < planes)
        def _():
            to_plane(d).start()

    pairs(cuts[1], cuts[2], local)

    a1 = a128[i] * a128[i]
    a4 = a1 * a1
    a4 = a4 * a4
    lead = jnp.ones_like(a4)
    for d in range(1, planes):
        lead = jnp.where(z >= d, lead * a4, lead)
    acc[...] = same(entry, jnp.zeros_like(entry)) * lead * carry_ref[:, lanes(i, wq)]
    power = jnp.ones_like(a4)
    for d in range(1, planes):
        @pl.when(z >= d)
        def _():
            to_plane(d).wait_recv()
            acc[...] += same(end_of(G * (z - d) + G - 1), entry) * power * xr[d].astype(F32)
        power = power * a4
    state = acc[...]
    s3[0] = state.astype(BF16)
    power = a1
    for k in range(1, G):
        held = same(ends[k - 1], entry) * power * state
        power = power * a1
        fall = None
        for b in range(k - 1, -1, -1):
            term = same(ends[b], ends[k - 1]) * b_ref[b].astype(F32)
            held = held + (term if fall is None else term * fall)
            fall = a1 if fall is None else fall * a1
        s3[k] = held.astype(BF16)

    def back(d):
        k = (i + d) % G
        return remote(s3.at[k], sin.at[i], s3_send.at[d], s3_recv.at[i], z * G + k)

    def back_from(d):
        k = (i + d) % G
        return remote(s3.at[k], sin.at[k], s3_send.at[d], s3_recv.at[k], z * G + k)

    for d in range(1, G):
        back(d).start()
    sin[i] = s3[i]

    pairs(cuts[2], cuts[3], local)

    for d in range(1, G):
        back_from(d).wait_recv()

    def emit(t):
        return pltpu.make_async_copy(outb.at[:, lanes(t)], out_hbm.at[:, lanes(t)], osem.at[t])

    def finish(t):
        at = lanes(t)
        state = sin[t // per, :, lanes(t % per)]
        later = keep_ref[0:1, 0:1] * a128[t // per, :, lanes(t % per)] * state.astype(F32) + s0_ref[:, at]
        for j, held in enumerate((state, later.astype(BF16))):
            rows = slice(j * L, (j + 1) * L)
            cross = mm(cw[rows, at], spread(held, diag16_ref[...]))
            outb[rows, at] = (part[rows, at] + cross).astype(BF16)
        emit(t).start()

    pairs(0, tiles, lambda t, slot: finish(t))

    @pl.when(p < n - 1)
    def _():
        tail_copy.wait_send()
    for d in range(1, G):
        to_mate(d).wait_send()
        back(d).wait_send()
    for d in range(1, planes):
        @pl.when(z + d < planes)
        def _():
            to_plane(d).wait_send()
    lax.fori_loop(0, tiles, lambda t, c: (emit(t).wait(), c)[1], 0)


def gate_kernel(seg_ref, feat_ref, first_ref, taps_ref, total_ref, out_ref, mask_ref, near_ref, cmask_ref, dmask_ref):
    @pl.when(pl.program_id(0) == 0)
    def _():
        segment_tables(seg_ref, lax.axis_index("ctx"), mask_ref, near_ref, cmask_ref, dmask_ref)

    for c in range(GW // W):
        at = slice(c * W, (c + 1) * W)
        q = short_filter(feat_ref[0, :, at].astype(F32), first_ref[0:2, at], taps_ref[:, 0, at], near_ref)
        out_ref[:, at] = (q * total_ref[:, at].astype(F32)).astype(BF16)


def body(features, short_weight, residues, rates, skip, carry_state, earlier_rows, segment_ids):
    count, _, width = features.shape
    groups, modes = rates.shape
    tiles = width // W
    wq = width // G
    n = lax.axis_size("ctx")
    planes = n // G
    vmem = pl.BlockSpec(memory_space=pltpu.VMEM)
    hbm = pl.BlockSpec(memory_space=pl.ANY)
    dma = pltpu.SemaphoreType.DMA
    seg = segment_ids.reshape(-1, L)
    feat = features.transpose(1, 0, 2)
    total, first = pl.pallas_call(
        functools.partial(kernel, n),
        in_specs=[vmem, hbm, vmem, vmem, vmem, vmem, vmem, vmem],
        out_specs=[hbm, vmem],
        out_shape=[jax.ShapeDtypeStruct((count, width), BF16), jax.ShapeDtypeStruct((8, width), F32)],
        scratch_shapes=[
            pltpu.VMEM((3, count, width), BF16),
            pltpu.VMEM((3, 16, width), BF16),
            pltpu.VMEM((16, width // 2), BF16),
            pltpu.VMEM((16, width // 2), BF16),
            pltpu.VMEM((3, 8, width), F32),
            pltpu.VMEM((count, L), BF16),
            pltpu.VMEM((2, count, L), F32),
            pltpu.VMEM((count, L), F32),
            pltpu.VMEM((8, L), F32),
            pltpu.VMEM((W, W), F32),
            pltpu.VMEM((W, W), BF16),
            pltpu.VMEM((16, L), F32),
            pltpu.VMEM((2, groups * modes, L), BF16),
            pltpu.VMEM((count, groups * modes), BF16),
            pltpu.VMEM((groups * FG, L), HS),
            pltpu.VMEM((G, modes, wq), F32),
            pltpu.VMEM((count, width), BF16),
            pltpu.VMEM((count, width), F32),
            pltpu.VMEM((modes, width), F32),
            pltpu.VMEM((G, modes, wq), BF16),
            pltpu.VMEM((G, modes, wq), BF16),
            pltpu.VMEM((modes, wq), BF16),
            pltpu.VMEM((planes, modes, wq), BF16),
            pltpu.VMEM((modes, wq), F32),
            pltpu.VMEM((G, modes, wq), BF16),
            pltpu.VMEM((G, modes, wq), BF16),
            pltpu.VMEM((2, 2, L, GT * L), BF16),
            pltpu.VMEM((2, 2, GT * L, W), BF16),
            pltpu.VMEM((count, width), BF16),
            dma((width // FW,)),
            dma, dma, dma,
            dma((G,)), dma((G,)),
            dma((planes,)), dma((planes,)),
            dma((G,)), dma((G,)),
            dma((tiles,)),
        ],
        compiler_params=pltpu.CompilerParams(
            collective_id=0, has_side_effects=True, vmem_limit_bytes=56 * 1024 * 1024),
        name="hyena",
    )(seg, feat, earlier_rows.transpose(1, 0, 2), short_weight,
      skip.reshape(1, -1), rates.T, residues.T, carry_state)
    whole = lambda shape: pl.BlockSpec(shape, lambda i: (0,) * len(shape))
    return pl.pallas_call(
        gate_kernel,
        grid=(width // GW,),
        in_specs=[
            whole(seg.shape),
            pl.BlockSpec((1, count, GW), lambda i: (0, 0, i)),
            pl.BlockSpec((8, GW), lambda i: (0, i)),
            pl.BlockSpec((3, 3, GW), lambda i: (0, 0, i)),
            pl.BlockSpec((count, GW), lambda i: (0, i)),
        ],
        out_specs=pl.BlockSpec((count, GW), lambda i: (0, i)),
        out_shape=jax.ShapeDtypeStruct((count, width), BF16),
        scratch_shapes=[
            pltpu.VMEM((count, L), BF16),
            pltpu.VMEM((2, count, L), F32),
            pltpu.VMEM((count, L), F32),
            pltpu.VMEM((8, L), F32),
        ],
        compiler_params=pltpu.CompilerParams(vmem_limit_bytes=56 * 1024 * 1024),
        name="gate",
    )(seg, feat, first, short_weight, total)


def solution(mesh):
    placed = (
        P(("groups", "ctx"), None, None),
        P(),
        P(),
        P(),
        P(),
        P("groups", None),
        P("groups", None, None),
        P("groups"),
    )
    return jax.shard_map(
        body, mesh=mesh, in_specs=placed, out_specs=P(("groups", "ctx"), None), check_vma=False
    )
```
